512 devices in a mesh: rows: 32 (over z, core), vocab: 16 (over x, y).
Axes of the slice: x: 4, y: 4, z: 16, core: 2. Of those that a mesh axis runs over, the one named last changes fastest.
Arguments:
- hidden: bfloat16 [1024, 5376], P('rows'), may hold values from -6 to 6
- logits: bfloat16 [1024, 131072], P(None, ('vocab', 'rows')), may hold values from -120 to 260
- eta: float32 [1024], replicated, may hold values from 0.0001 to 0.003
- teacher: int32 [1024], replicated, may hold values from 0 to 131071
- valid: int32 [1024], replicated, may hold values 0 or 1
Outputs:
- head_grad: bfloat16 [131072, 5376], P(('vocab', 'rows'))
- row_loss: float32 [1024], P(('rows', 'vocab'))
The draws below stay inside these ranges and needn't reach their ends.
All inputs are finite; a program needn't handle non-finite values.
Results may differ from the reference program's by a relative error of at most 0.0028.
Values may be sent and summed in bfloat16 or wider, within the bound.
No kernel may reach another device: no remote copies, remote signals or barrier semaphores. Data moves between devices by JAX's collectives and lax.ppermute only.
A program may use at most 64 MiB of HBM per device.

```python
import math
import jax
import jax.numpy as jnp
from jax import lax

D = 5376
VOCAB_DEV = 256
ROWS = 1024
VOCAB = 131072


def draw_logits(key, part):
    key = jax.random.fold_in(key, 7)
    keys = jax.random.split(key, 3)
    row_scale = jnp.exp(jax.random.uniform(keys[0], (ROWS, 1), minval=math.log(2.5), maxval=math.log(12.0)))
    values = jax.random.normal(keys[2], (ROWS, VOCAB)) * row_scale
    return jnp.clip(values, -120.0, 260.0).astype(jnp.bfloat16)


def plant(entries, own_key, smallest, top_value):
    place = [jax.random.randint(jax.random.fold_in(own_key, axis), (), 0, length) for axis, length in enumerate(entries.shape)]
    widest = entries.shape.index(max(entries.shape))
    beside = place[:widest] + [(place[widest] + 1) % entries.shape[widest]] + place[widest + 1:]
    return entries.at[tuple(place)].set(smallest).at[tuple(beside)].set(top_value)


def steps_of(key, shape, cuts, least, high):
    factor_of = 1.0
    for axis_at, parts in cuts:
        heights = jax.random.uniform(jax.random.fold_in(jax.random.fold_in(key, 6), axis_at), (parts,), jnp.float32, least / len(cuts), high / len(cuts))
        factor_of = factor_of * jnp.repeat(jnp.exp(heights), shape[axis_at] // parts).reshape((-1,) + (1,) * (len(shape) - 1 - axis_at))
    return factor_of


def scatter_about(stream_key, dims, width, reach, cuts=(), held_as=jnp.bfloat16):
    entries = jax.random.normal(stream_key, dims, jnp.float32) * width
    if len(cuts) > 0:
        entries = steps_of(stream_key, dims, cuts, -0.22, 0.18) * entries
    return jnp.clip(entries, min=-reach, max=reach).astype(held_as)


def setup_inputs(seed: int = 0) -> dict:
    key_of = jax.random.split(jax.random.key(seed), 6)
    return {
        "hidden": scatter_about(key_of[0], (ROWS, D), 1.0, 6.0, ((0, 32),)),
        "logits": draw_logits(jax.random.fold_in(key_of[5], 71), 0),
        "eta": jnp.clip(jnp.exp(jax.random.uniform(key_of[2], (ROWS,), jnp.float32, math.log(0.0001), math.log(0.003))), 0.0001, 0.003),
        "teacher": plant(jax.random.randint(key_of[3], (ROWS,), 0, VOCAB), jax.random.fold_in(key_of[3], 1), 0, VOCAB - 1).astype(jnp.int32),
        "valid": plant((jax.random.randint(key_of[4], (ROWS,), 0, 4) < 3).astype(jnp.int32), jax.random.fold_in(key_of[4], 1), 0, 1),
    }


def reference(hidden, logits, eta, teacher, valid):
    z = logits.astype(jnp.float32)
    peak = lax.optimization_barrier(jnp.max(z, axis=1))
    e = jnp.exp(z - peak[:, None])
    total = lax.optimization_barrier(jnp.sum(e, axis=1))
    spread = lax.optimization_barrier(jnp.sum(e * (z - peak[:, None]), axis=1))
    entropy = jnp.log(total) - spread / total
    cutoff = jnp.minimum(eta, jnp.sqrt(eta) * jnp.exp(-entropy))
    columns = jnp.arange(VOCAB, dtype=jnp.int32)
    chosen = columns[None, :] == teacher[:, None]
    kept = jnp.where((e > (cutoff * total)[:, None]) | chosen, e, jnp.float32(0.0))
    mass = lax.optimization_barrier(jnp.sum(kept, axis=1))
    target = lax.optimization_barrier(jnp.sum(jnp.where(chosen, z, jnp.float32(0.0)), axis=1))
    live = valid.astype(jnp.float32)
    row_loss = live * (jnp.log(mass) + peak - target)
    grads = (live[:, None] * (kept / mass[:, None] - chosen.astype(jnp.float32))).astype(jnp.bfloat16)
    blocks = VOCAB // VOCAB_DEV
    stacked = grads.reshape(ROWS, blocks, VOCAB_DEV).transpose(1, 0, 2)

    def one_block(block):
        product = lax.dot_general(block, hidden, (((0,), (0,)), ((), ())), preferred_element_type=jnp.float32)
        return product.astype(jnp.bfloat16)
    head_grad = lax.map(one_block, stacked).reshape(VOCAB, D)
    return (head_grad, row_loss)
```

```python
import functools

import jax
import jax.numpy as jnp
from jax import lax
from jax.experimental import pallas as pl
from jax.experimental.pallas import tpu as pltpu
from jax.sharding import PartitionSpec as P

LANES = 128
F32 = jnp.float32


def local_stats(copies, logits_ref, rel_ref, zt_ref, out_ref, stat):
    groups = logits_ref.shape[0] // LANES
    for i in range(groups):
        z = logits_ref[i * LANES : (i + 1) * LANES, :].astype(F32).T
        zt_ref[:, i * LANES : (i + 1) * LANES] = z.astype(jnp.bfloat16)
        peak = jnp.max(z, axis=0, keepdims=True)
        below = z - peak
        e = jnp.exp(below)
        chosen = lax.broadcasted_iota(jnp.int32, z.shape, 0) == rel_ref[i : i + 1, :]
        stat[i : i + 1, :] = peak
        stat[groups + i : groups + i + 1, :] = jnp.sum(e, axis=0, keepdims=True)
        stat[2 * groups + i : 2 * groups + i + 1, :] = jnp.sum(e * below, axis=0, keepdims=True)
        stat[3 * groups + i : 3 * groups + i + 1, :] = jnp.sum(
            jnp.where(chosen, z, 0.0), axis=0, keepdims=True
        )
    for j in range(copies):
        out_ref[j] = stat[...]


def merged(parts_ref):
    n, depth, _ = parts_ref.shape
    g = depth // 4
    peak = parts_ref[0, :g, :]
    for j in range(1, n):
        peak = jnp.maximum(peak, parts_ref[j, :g, :])
    total = jnp.zeros_like(peak)
    spread = jnp.zeros_like(peak)
    target = jnp.zeros_like(peak)
    for j in range(n):
        gap = parts_ref[j, :g, :] - peak
        scale = jnp.exp(gap)
        part = parts_ref[j, g : 2 * g, :]
        total += scale * part
        spread += scale * (parts_ref[j, 2 * g : 3 * g, :] + gap * part)
        target += parts_ref[j, 3 * g :, :]
    return peak, total, spread, target


def merge_stats(copies, parts_ref, out_ref):
    peak, total, spread, target = merged(parts_ref)
    g = peak.shape[0]
    for j in range(copies):
        out_ref[j, :g, :] = peak
        out_ref[j, g : 2 * g, :] = total
        out_ref[j, 2 * g : 3 * g, :] = spread
        out_ref[j, 3 * g :, :] = target


def kept_of(zt_ref, i, peak, limit, rel):
    z = zt_ref[:, i * LANES : (i + 1) * LANES].astype(F32)
    e = jnp.exp(z - peak)
    chosen = lax.broadcasted_iota(jnp.int32, z.shape, 0) == rel
    return jnp.where((e > limit) | chosen, e, 0.0), chosen


def local_mass(copies, parts_ref, zt_ref, eta_ref, rel_ref, row_ref, out_ref, mass):
    peak, total, spread, target = merged(parts_ref)
    g = peak.shape[0]
    eta = eta_ref[...]
    entropy = jnp.log(total) - spread / total
    cutoff = jnp.minimum(eta, jnp.sqrt(eta) * jnp.exp(-entropy))
    row_ref[0] = peak
    row_ref[1] = cutoff * total
    row_ref[2] = target
    for i in range(g):
        at = slice(i, i + 1)
        kept, _ = kept_of(zt_ref, i, row_ref[0, at, :], row_ref[1, at, :], rel_ref[at, :])
        mass[at, :] = jnp.sum(kept, axis=0, keepdims=True)
    for j in range(copies):
        out_ref[j] = mass[...]


def merge_mass(copies, parts_ref, out_ref):
    mass = parts_ref[0]
    for j in range(1, parts_ref.shape[0]):
        mass += parts_ref[j]
    for j in range(copies):
        out_ref[j] = mass


def head_grad_kernel(
    parts_ref, row_ref, zt_ref, rel_ref, valid_ref, own_ref, hidden_ref, out_ref, loss_ref, mass, grads
):
    @pl.when(pl.program_id(0) == 0)
    def _():
        total = parts_ref[0]
        for j in range(1, parts_ref.shape[0]):
            total += parts_ref[j]
        mass[...] = total
        g = total.shape[0]
        live = valid_ref[...].astype(F32)
        loss = live * (jnp.log(total) + row_ref[0] - row_ref[2])
        place = lax.broadcasted_iota(jnp.int32, loss.shape, 0) * LANES + lax.broadcasted_iota(
            jnp.int32, loss.shape, 1
        )
        for k in range(loss_ref.shape[0]):
            loss_ref[k] = jnp.sum(jnp.where(place == own_ref[0] + k, loss, 0.0))
        for i in range(g):
            at = slice(i, i + 1)
            kept, chosen = kept_of(zt_ref, i, row_ref[0, at, :], row_ref[1, at, :], rel_ref[at, :])
            grads[:, i * LANES : (i + 1) * LANES] = (
                live[at, :] * (kept / mass[at, :] - chosen.astype(F32))
            ).astype(jnp.bfloat16)

    out_ref[...] = jnp.dot(grads[...], hidden_ref[...], preferred_element_type=F32).astype(
        out_ref.dtype
    )


VMEM = pl.BlockSpec(memory_space=pltpu.VMEM)
SMEM = pl.BlockSpec(memory_space=pltpu.SMEM)


def call(kernel, outs, scratch, flops, *args):
    moved = sum(a.size * a.dtype.itemsize for a in args) + sum(
        o.size * o.dtype.itemsize for o in jax.tree.leaves(outs)
    )
    return pl.pallas_call(
        kernel,
        out_shape=outs,
        in_specs=[VMEM] * len(args),
        out_specs=jax.tree.map(lambda _: VMEM, outs),
        scratch_shapes=scratch,
        compiler_params=pltpu.CompilerParams(vmem_limit_bytes=24 << 20),
        cost_estimate=pl.CostEstimate(flops=flops, bytes_accessed=moved, transcendentals=0),
    )(*args)


def spread_out(parts, axis):
    return lax.all_to_all(parts, axis, split_axis=0, concat_axis=0, tiled=True)


def per_device(hidden, logits, eta, teacher, valid):
    n_rows, n_vocab = lax.axis_size("rows"), lax.axis_size("vocab")
    rows, wide = logits.shape
    width = hidden.shape[1]
    g = rows // LANES
    whole = lax.all_gather(hidden, "rows", axis=0, tiled=True)
    at_rows, at_vocab = lax.axis_index("rows"), lax.axis_index("vocab")
    rel = (teacher - (at_vocab * n_rows + at_rows) * wide).reshape(g, LANES)
    share = rows // (n_rows * n_vocab)
    own = ((at_rows * n_vocab + at_vocab) * share).reshape(1)
    shape = jax.ShapeDtypeStruct

    zt, parts = call(
        functools.partial(local_stats, n_vocab),
        (shape((wide, rows), jnp.bfloat16), shape((n_vocab, 4 * g, LANES), F32)),
        [pltpu.VMEM((4 * g, LANES), F32)],
        20 * rows * wide,
        logits,
        rel,
    )
    parts = spread_out(parts, "vocab")
    parts = call(
        functools.partial(merge_stats, n_rows), shape((n_rows, 4 * g, LANES), F32), [], rows * 128, parts
    )
    parts = spread_out(parts, "rows")
    row_stats, masses = call(
        functools.partial(local_mass, n_vocab),
        (shape((3, g, LANES), F32), shape((n_vocab, g, LANES), F32)),
        [pltpu.VMEM((g, LANES), F32)],
        20 * rows * wide,
        parts,
        zt,
        eta.reshape(g, LANES),
        rel,
    )
    masses = spread_out(masses, "vocab")
    masses = call(
        functools.partial(merge_mass, n_rows), shape((n_rows, g, LANES), F32), [], rows * 16, masses
    )
    masses = spread_out(masses, "rows")

    tile = 768
    head_grad, row_loss = pl.pallas_call(
        head_grad_kernel,
        grid=(width // tile,),
        in_specs=[VMEM] * 5 + [SMEM, pl.BlockSpec((rows, tile), lambda j: (0, j))],
        out_specs=(pl.BlockSpec((wide, tile), lambda j: (0, j)), SMEM),
        out_shape=(shape((wide, width), jnp.bfloat16), shape((share,), F32)),
        scratch_shapes=[pltpu.VMEM((g, LANES), F32), pltpu.VMEM((wide, rows), jnp.bfloat16)],
        compiler_params=pltpu.CompilerParams(vmem_limit_bytes=56 << 20),
        cost_estimate=pl.CostEstimate(
            flops=2 * rows * wide * width,
            bytes_accessed=2 * (rows * width + wide * width),
            transcendentals=0,
        ),
    )(masses, row_stats, zt, rel, valid.reshape(g, LANES), own, whole)
    return head_grad, row_loss


def solution(mesh):
    placed = (P("rows", None), P(None, ("vocab", "rows")), P(), P(), P())
    return jax.shard_map(
        per_device,
        mesh=mesh,
        in_specs=placed,
        out_specs=(P(("vocab", "rows"), None), P(("rows", "vocab"))),
        check_vma=False,
    )
```

```python
import functools

import jax
import jax.numpy as jnp
from jax import lax
from jax.experimental import pallas as pl
from jax.experimental.pallas import tpu as pltpu
from jax.sharding import Mesh
from jax.sharding import PartitionSpec as P

LANES = 128
F32 = jnp.float32
PEAK, TOTAL, SPREAD, TARGET, MASS = range(5)


def turned(columns):
    n = columns[0].shape[0]
    lane = lax.broadcasted_iota(jnp.int32, (n, LANES), 1)
    x = jnp.zeros((n, LANES), F32)
    for k, c in enumerate(columns):
        x = jnp.where(lane == k, c, x)
    x = jnp.concatenate([x, jnp.zeros((LANES - n, LANES), F32)], axis=0)
    return x.T[:8, :]


def chosen_at(teacher, source, z_at, n_z, shape):
    width = shape[1]
    base = ((source // 2 * n_z + z_at) * 2 + source % 2) * width
    return lax.broadcasted_iota(jnp.int32, shape, 1) + base == teacher


def share_stats(n_z, at_ref, logits_ref, teacher_ref, out_ref):
    n, rows, wide = logits_ref.shape
    half = wide // LANES
    teacher = teacher_ref[...]

    def block(s):
        return logits_ref[s].astype(F32)

    top = block(0)
    for s in range(1, n):
        top = jnp.maximum(top, block(s))
    peak = jnp.max(top, axis=1, keepdims=True)
    total = jnp.zeros((rows, wide), F32)
    spread = jnp.zeros((rows, wide), F32)
    target = jnp.zeros((rows, wide), F32)
    for s in range(n):
        z = block(s)
        below = z - peak
        e = jnp.exp(below)
        total += e
        spread += e * below
        target += jnp.where(chosen_at(teacher, s, at_ref[0], n_z, z.shape), z, 0.0)
    tile = turned([peak] + [jnp.sum(x, axis=1, keepdims=True) for x in (total, spread, target)])
    for j in range(out_ref.shape[0]):
        out_ref[j] = tile


def share_mass(n_z, at_ref, parts_ref, logits_ref, teacher_ref, eta_ref, row_ref, out_ref):
    n, rows, wide = logits_ref.shape
    parts = [parts_ref[j] for j in range(parts_ref.shape[0])]
    peak = parts[0][PEAK : PEAK + 1]
    for p in parts[1:]:
        peak = jnp.maximum(peak, p[PEAK : PEAK + 1])
    total = jnp.zeros_like(peak)
    spread = jnp.zeros_like(peak)
    target = jnp.zeros_like(peak)
    for p in parts:
        gap = p[PEAK : PEAK + 1] - peak
        scale = jnp.exp(gap)
        total += scale * p[TOTAL : TOTAL + 1]
        spread += scale * (p[SPREAD : SPREAD + 1] + gap * p[TOTAL : TOTAL + 1])
        target += p[TARGET : TARGET + 1]
    lane = lax.broadcasted_iota(jnp.int32, total.shape, 1)
    total = jnp.where(lane < rows, total, 1.0)
    eta = eta_ref[...]
    entropy = jnp.log(total) - spread / total
    cutoff = jnp.minimum(eta, jnp.sqrt(eta) * jnp.exp(-entropy))
    limit = cutoff * total
    tile = jnp.concatenate([peak, limit, target, jnp.zeros((5, LANES), F32)], axis=0)
    row_ref[...] = tile
    columns = jnp.concatenate([tile, jnp.zeros((LANES - 8, LANES), F32)], axis=0).T
    peak_c, limit_c = columns[:rows, 0:1], columns[:rows, 1:2]
    teacher = teacher_ref[...]
    mass = jnp.zeros((rows, wide), F32)
    for s in range(n):
        e = jnp.exp(logits_ref[s].astype(F32) - peak_c)
        chosen = chosen_at(teacher, s, at_ref[0], n_z, e.shape)
        mass += jnp.where((e > limit_c) | chosen, e, 0.0)
    tile = turned([jnp.sum(mass, axis=1, keepdims=True)])
    for j in range(out_ref.shape[0]):
        out_ref[j] = tile


def finish_rows(rows, at_ref, masses_ref, row_ref, out_ref):
    mass = masses_ref[0][:1]
    for j in range(1, masses_ref.shape[0]):
        mass += masses_ref[j][:1]
    row = row_ref[...]
    tile = jnp.concatenate([row[:3], mass, row[4:]], axis=0)
    lane = lax.broadcasted_iota(jnp.int32, tile.shape, 1)
    tile = jnp.where(lane < rows, tile, 0.0)
    per = LANES // rows
    placed = jnp.zeros_like(tile)
    for k in range(per):
        moved = pltpu.roll(tile, k * rows, 1) if k else tile
        placed = jnp.where(at_ref[0] % per == k, moved, placed)
    for j in range(out_ref.shape[0]):
        out_ref[j] = placed


def turn_logits(logits_ref, zt_ref):
    for i in range(logits_ref.shape[0] // LANES):
        at = slice(i * LANES, (i + 1) * LANES)
        zt_ref[:, at] = logits_ref[at, :].astype(F32).T.astype(jnp.bfloat16)


def logit_grads(own_ref, rows_ref, zt_ref, rel_ref, valid_ref, grads_ref, loss_ref):
    groups = zt_ref.shape[1] // LANES
    per = rows_ref.shape[0] // groups
    loss = [jnp.float32(0.0) for _ in range(loss_ref.shape[0])]
    for i in range(groups):
        tile = rows_ref[per * i]
        for k in range(1, per):
            tile += rows_ref[per * i + k]
        peak, limit, target, mass = (tile[k : k + 1] for k in range(4))
        live = valid_ref[i : i + 1, :].astype(F32)
        row_loss = live * (jnp.log(mass) + peak - target)
        place = lax.broadcasted_iota(jnp.int32, row_loss.shape, 1) + i * LANES
        for k in range(len(loss)):
            loss[k] += jnp.sum(jnp.where(place == own_ref[0] + k, row_loss, 0.0))
        at = slice(i * LANES, (i + 1) * LANES)
        z = zt_ref[:, at].astype(F32)
        e = jnp.exp(z - peak)
        chosen = lax.broadcasted_iota(jnp.int32, z.shape, 0) == rel_ref[i : i + 1, :]
        kept = jnp.where((e > limit) | chosen, e, 0.0)
        grads_ref[:, at] = (live * (kept / mass - chosen.astype(F32))).astype(jnp.bfloat16)
    for k in range(len(loss)):
        loss_ref[k] = loss[k]


def head_product(grads_ref, hidden_ref, out_ref):
    out_ref[...] = jnp.dot(grads_ref[...], hidden_ref[...], preferred_element_type=F32).astype(
        out_ref.dtype
    )


VMEM = pl.BlockSpec(memory_space=pltpu.VMEM)
SMEM = pl.BlockSpec(memory_space=pltpu.SMEM)


def call(kernel, outs, flops, *args, in_specs=None, out_specs=None):
    moved = sum(a.size * a.dtype.itemsize for a in args) + sum(
        o.size * o.dtype.itemsize for o in jax.tree.leaves(outs)
    )
    return pl.pallas_call(
        kernel,
        out_shape=outs,
        in_specs=in_specs or [SMEM if a.shape == (1,) else VMEM for a in args],
        out_specs=out_specs or jax.tree.map(lambda _: VMEM, outs),
        compiler_params=pltpu.CompilerParams(vmem_limit_bytes=24 << 20),
        cost_estimate=pl.CostEstimate(flops=flops, bytes_accessed=moved, transcendentals=0),
    )(*args)


def swap(parts, axis):
    return lax.all_to_all(parts, axis, split_axis=0, concat_axis=0, tiled=True)


def per_device(hidden, logits, eta, teacher, valid):
    n_z, n_vocab = lax.axis_size("z"), lax.axis_size("vocab")
    plane = ("vocab", "core")
    n_plane = 2 * n_vocab
    rows, wide = logits.shape
    width = hidden.shape[1]
    g = rows // LANES
    mine = rows // n_plane
    share = rows // (n_z * n_plane)
    shape = jax.ShapeDtypeStruct
    at_z, at_core, at_vocab = (lax.axis_index(a) for a in ("z", "core", "vocab"))
    at_plane = at_vocab * 2 + at_core

    whole = lax.all_gather(hidden, ("z", "core"), axis=0, tiled=True)

    mine_logits = swap(logits.reshape(n_plane, mine, wide), plane)
    zt = call(turn_logits, shape((wide, rows), jnp.bfloat16), rows * wide, logits)
    my_teacher = lax.dynamic_slice_in_dim(teacher, at_plane * mine, mine).reshape(mine, 1)
    my_eta = lax.dynamic_slice_in_dim(eta, at_plane * mine, mine)
    my_eta = jnp.pad(my_eta, (0, LANES - mine), constant_values=0.001).reshape(1, LANES)
    z_one = at_z.reshape(1)
    tiles = shape((n_z, 8, LANES), F32)
    parts = call(
        functools.partial(share_stats, n_z), tiles, 20 * rows * wide, z_one, mine_logits, my_teacher
    )
    row_stats, masses = call(
        functools.partial(share_mass, n_z),
        (shape((8, LANES), F32), tiles),
        20 * rows * wide,
        z_one,
        swap(parts, "z"),
        mine_logits,
        my_teacher,
        my_eta,
    )
    done = call(
        functools.partial(finish_rows, mine),
        shape((n_plane, 8, LANES), F32),
        rows * 16,
        at_plane.reshape(1),
        swap(masses, "z"),
        row_stats,
    )
    done = swap(done, plane)
    rel = (teacher - ((at_vocab * n_z + at_z) * 2 + at_core) * wide).reshape(g, LANES)
    own = (((at_z * 2 + at_core) * n_vocab + at_vocab) * share).reshape(1)
    grads, row_loss = call(
        logit_grads,
        (shape((wide, rows), jnp.bfloat16), shape((share,), F32)),
        20 * rows * wide,
        own,
        done,
        zt,
        rel,
        valid.reshape(g, LANES),
        out_specs=(VMEM, SMEM),
    )

    tile = 768
    head_grad = pl.pallas_call(
        head_product,
        grid=(width // tile,),
        in_specs=[VMEM, pl.BlockSpec((rows, tile), lambda j: (0, j))],
        out_specs=pl.BlockSpec((wide, tile), lambda j: (0, j)),
        out_shape=shape((wide, width), jnp.bfloat16),
        compiler_params=pltpu.CompilerParams(vmem_limit_bytes=56 << 20),
        cost_estimate=pl.CostEstimate(
            flops=2 * rows * wide * width,
            bytes_accessed=2 * (rows * width + wide * width),
            transcendentals=0,
        ),
    )(grads, whole)
    return head_grad, row_loss


def solution(mesh):
    n_rows, n_vocab = mesh.devices.shape
    split = Mesh(mesh.devices.reshape(n_rows // 2, 2, n_vocab), ("z", "core", "vocab"))
    rows, entries = ("z", "core"), ("vocab", "z", "core")
    return jax.shard_map(
        per_device,
        mesh=split,
        in_specs=(P(rows, None), P(None, entries), P(), P(), P()),
        out_specs=(P(entries, None), P(("z", "core", "vocab"))),
        check_vma=False,
    )
```

```python
import functools

import jax
import jax.numpy as jnp
from jax import lax
from jax.experimental import pallas as pl
from jax.experimental.pallas import tpu as pltpu
from jax.sharding import Mesh
from jax.sharding import PartitionSpec as P

LANES = 128
F32 = jnp.float32


def turned(columns):
    n = columns[0].shape[0]
    lane = lax.broadcasted_iota(jnp.int32, (n, LANES), 1)
    x = jnp.zeros((n, LANES), F32)
    for k, c in enumerate(columns):
        x = jnp.where(lane == k, c, x)
    x = jnp.concatenate([x, jnp.zeros((LANES - n, LANES), F32)], axis=0)
    x = x.T[:8, :]
    lane = lax.broadcasted_iota(jnp.int32, (1, LANES), 1)
    row = jnp.zeros((1, LANES), F32)
    for k in range(len(columns)):
        moved = pltpu.roll(x[k : k + 1], k * n, 1) if k else x[:1]
        row = jnp.where(lane // n == k, moved, row)
    return row


def chosen_at(teacher, source, z_at, n_z, shape):
    width = shape[1]
    base = ((source // 2 * n_z + z_at) * 2 + source % 2) * width
    return lax.broadcasted_iota(jnp.int32, shape, 1) + base == teacher


def share_stats(n_z, at_ref, logits_ref, teacher_ref, out_ref):
    n, rows, wide = logits_ref.shape
    half = wide // LANES
    teacher = teacher_ref[...]

    def block(s):
        return logits_ref[s].astype(F32)

    top = block(0)
    for s in range(1, n):
        top = jnp.maximum(top, block(s))
    peak = jnp.max(top, axis=1, keepdims=True)
    total = jnp.zeros((rows, wide), F32)
    spread = jnp.zeros((rows, wide), F32)
    target = jnp.zeros((rows, wide), F32)
    for s in range(n):
        z = block(s)
        below = z - peak
        e = jnp.exp(below)
        total += e
        spread += e * below
        target += jnp.where(chosen_at(teacher, s, at_ref[0], n_z, z.shape), z, 0.0)
    tile = turned([peak] + [jnp.sum(x, axis=1, keepdims=True) for x in (total, spread, target)])
    for j in range(out_ref.shape[0]):
        out_ref[j] = tile


def share_mass(n_z, at_ref, parts_ref, logits_ref, teacher_ref, eta_ref, row_ref, out_ref):
    n, rows, wide = logits_ref.shape
    parts = jnp.concatenate([parts_ref[j] for j in range(parts_ref.shape[0])], axis=0)
    tops, totals, spreads, targets = (
        pltpu.roll(parts, LANES - k * rows, 1) if k else parts for k in range(4)
    )
    peak = jnp.max(tops, axis=0, keepdims=True)
    gap = tops - peak
    scale = jnp.exp(jnp.minimum(gap, 0.0))
    total = jnp.sum(scale * totals, axis=0, keepdims=True)
    spread = jnp.sum(scale * (spreads + gap * totals), axis=0, keepdims=True)
    target = jnp.sum(targets, axis=0, keepdims=True)
    lane = lax.broadcasted_iota(jnp.int32, total.shape, 1)
    total = jnp.where(lane < rows, total, 1.0)
    eta = eta_ref[...]
    entropy = jnp.log(total) - spread / total
    cutoff = jnp.minimum(eta, jnp.sqrt(eta) * jnp.exp(-entropy))
    limit = cutoff * total
    tile = jnp.concatenate([peak, limit, target, jnp.zeros((5, LANES), F32)], axis=0)
    row_ref[...] = tile
    columns = jnp.concatenate([tile, jnp.zeros((LANES - 8, LANES), F32)], axis=0).T
    peak_c, limit_c = columns[:rows, 0:1], columns[:rows, 1:2]
    teacher = teacher_ref[...]
    mass = jnp.zeros((rows, wide), F32)
    for s in range(n):
        e = jnp.exp(logits_ref[s].astype(F32) - peak_c)
        chosen = chosen_at(teacher, s, at_ref[0], n_z, e.shape)
        mass += jnp.where((e > limit_c) | chosen, e, 0.0)
    tile = turned([jnp.sum(mass, axis=1, keepdims=True)])
    for j in range(out_ref.shape[0]):
        out_ref[j] = tile


def finish_rows(rows, at_ref, masses_ref, row_ref, out_ref):
    mass = masses_ref[0]
    for j in range(1, masses_ref.shape[0]):
        mass += masses_ref[j]
    row = row_ref[...]
    tile = jnp.concatenate([row[:3], mass, row[4:]], axis=0)
    lane = lax.broadcasted_iota(jnp.int32, tile.shape, 1)
    tile = jnp.where(lane < rows, tile, 0.0)
    per = LANES // rows
    placed = jnp.zeros_like(tile)
    for k in range(per):
        moved = pltpu.roll(tile, k * rows, 1) if k else tile
        placed = jnp.where(at_ref[0] % per == k, moved, placed)
    for j in range(out_ref.shape[0]):
        out_ref[j] = placed


def turn_logits(logits_ref, zt_ref):
    for i in range(logits_ref.shape[0] // LANES):
        at = slice(i * LANES, (i + 1) * LANES)
        zt_ref[:, at] = logits_ref[at, :].astype(F32).T.astype(jnp.bfloat16)


def logit_grads(own_ref, rows_ref, zt_ref, rel_ref, valid_ref, grads_ref, loss_ref):
    groups = zt_ref.shape[1] // LANES
    per = rows_ref.shape[0] // groups
    loss = [jnp.float32(0.0) for _ in range(loss_ref.shape[0])]
    for i in range(groups):
        tile = rows_ref[per * i]
        for k in range(1, per):
            tile += rows_ref[per * i + k]
        peak, limit, target, mass = (tile[k : k + 1] for k in range(4))
        live = valid_ref[i : i + 1, :].astype(F32)
        row_loss = live * (jnp.log(mass) + peak - target)
        place = lax.broadcasted_iota(jnp.int32, row_loss.shape, 1) + i * LANES
        for k in range(len(loss)):
            loss[k] += jnp.sum(jnp.where(place == own_ref[0] + k, row_loss, 0.0))
        at = slice(i * LANES, (i + 1) * LANES)
        z = zt_ref[:, at].astype(F32)
        e = jnp.exp(z - peak)
        chosen = lax.broadcasted_iota(jnp.int32, z.shape, 0) == rel_ref[i : i + 1, :]
        kept = jnp.where((e > limit) | chosen, e, 0.0)
        grads_ref[:, at] = (live * (kept / mass - chosen.astype(F32))).astype(jnp.bfloat16)
    for k in range(len(loss)):
        loss_ref[k] = loss[k]


def head_product(widths, ahead, grads_ref, hidden_ref, out_ref, held, result, in_sems, out_sems):
    starts = [sum(widths[:i]) for i in range(len(widths))]
    at = [pl.ds(s, w) for s, w in zip(starts, widths)]
    into = [
        pltpu.make_async_copy(hidden_ref.at[:, a], held.at[:, a], in_sems.at[i])
        for i, a in enumerate(at)
    ]
    out = [
        pltpu.make_async_copy(result.at[:, a], out_ref.at[:, a], out_sems.at[i])
        for i, a in enumerate(at)
    ]
    for copy in into[:ahead]:
        copy.start()
    for i, (s, w) in enumerate(zip(starts, widths)):
        into[i].wait()
        if i + ahead < len(widths):
            into[i + ahead].start()
        result[:, s : s + w] = jnp.dot(
            grads_ref[...], held[:, s : s + w], preferred_element_type=F32
        ).astype(result.dtype)
        out[i].start()
    for copy in out:
        copy.wait()


VMEM = pl.BlockSpec(memory_space=pltpu.VMEM)
SMEM = pl.BlockSpec(memory_space=pltpu.SMEM)


def call(kernel, outs, flops, *args, in_specs=None, out_specs=None):
    moved = sum(a.size * a.dtype.itemsize for a in args) + sum(
        o.size * o.dtype.itemsize for o in jax.tree.leaves(outs)
    )
    return pl.pallas_call(
        kernel,
        out_shape=outs,
        in_specs=in_specs or [SMEM if a.shape == (1,) else VMEM for a in args],
        out_specs=out_specs or jax.tree.map(lambda _: VMEM, outs),
        compiler_params=pltpu.CompilerParams(vmem_limit_bytes=24 << 20),
        cost_estimate=pl.CostEstimate(flops=flops, bytes_accessed=moved, transcendentals=0),
    )(*args)


def swap(parts, axis):
    return lax.all_to_all(parts, axis, split_axis=0, concat_axis=0, tiled=True)


def per_device(hidden, logits, eta, teacher, valid):
    n_z, n_vocab = lax.axis_size("z"), lax.axis_size("vocab")
    plane = ("vocab", "core")
    n_plane = 2 * n_vocab
    rows, wide = logits.shape
    width = hidden.shape[1]
    g = rows // LANES
    mine = rows // n_plane
    share = rows // (n_z * n_plane)
    shape = jax.ShapeDtypeStruct
    at_z, at_core, at_vocab = (lax.axis_index(a) for a in ("z", "core", "vocab"))
    at_plane = at_vocab * 2 + at_core

    whole = lax.all_gather(hidden, ("z", "core"), axis=0, tiled=True)

    mine_logits = swap(logits.reshape(n_plane, mine, wide), plane)
    zt = call(turn_logits, shape((wide, rows), jnp.bfloat16), rows * wide, logits)
    my_teacher = lax.dynamic_slice_in_dim(teacher, at_plane * mine, mine).reshape(mine, 1)
    my_eta = lax.dynamic_slice_in_dim(eta, at_plane * mine, mine)
    my_eta = jnp.pad(my_eta, (0, LANES - mine), constant_values=0.001).reshape(1, LANES)
    z_one = at_z.reshape(1)
    tiles = shape((n_z, 1, LANES), F32)
    parts = call(
        functools.partial(share_stats, n_z), tiles, 20 * rows * wide, z_one, mine_logits, my_teacher
    )
    row_stats, masses = call(
        functools.partial(share_mass, n_z),
        (shape((8, LANES), F32), tiles),
        20 * rows * wide,
        z_one,
        swap(parts, "z"),
        mine_logits,
        my_teacher,
        my_eta,
    )
    done = call(
        functools.partial(finish_rows, mine),
        shape((n_plane, 8, LANES), F32),
        rows * 16,
        at_plane.reshape(1),
        swap(masses, "z"),
        row_stats,
    )
    done = swap(done, plane)
    rel = (teacher - ((at_vocab * n_z + at_z) * 2 + at_core) * wide).reshape(g, LANES)
    own = (((at_z * 2 + at_core) * n_vocab + at_vocab) * share).reshape(1)
    grads, row_loss = call(
        logit_grads,
        (shape((wide, rows), jnp.bfloat16), shape((share,), F32)),
        20 * rows * wide,
        own,
        done,
        zt,
        rel,
        valid.reshape(g, LANES),
        out_specs=(VMEM, SMEM),
    )

    widths, left = [512], width - 512
    while left:
        widths.append(min(1024, left))
        left -= widths[-1]
    any_space = pl.BlockSpec(memory_space=pl.ANY)
    head_grad = pl.pallas_call(
        functools.partial(head_product, widths, 3),
        in_specs=[VMEM, any_space],
        out_specs=any_space,
        out_shape=shape((wide, width), jnp.bfloat16),
        scratch_shapes=[
            pltpu.VMEM((rows, width), jnp.bfloat16),
            pltpu.VMEM((wide, width), jnp.bfloat16),
            pltpu.SemaphoreType.DMA((len(widths),)),
            pltpu.SemaphoreType.DMA((len(widths),)),
        ],
        compiler_params=pltpu.CompilerParams(vmem_limit_bytes=56 << 20),
        cost_estimate=pl.CostEstimate(
            flops=2 * rows * wide * width,
            bytes_accessed=2 * (rows * width + wide * width),
            transcendentals=0,
        ),
    )(grads, whole)
    return head_grad, row_loss


def solution(mesh):
    n_rows, n_vocab = mesh.devices.shape
    split = Mesh(mesh.devices.reshape(n_rows // 2, 2, n_vocab), ("z", "core", "vocab"))
    rows, entries = ("z", "core"), ("vocab", "z", "core")
    return jax.shard_map(
        per_device,
        mesh=split,
        in_specs=(P(rows, None), P(None, entries), P(), P(), P()),
        out_specs=(P(entries, None), P(("z", "core", "vocab"))),
        check_vma=False,
    )
```

```python
import functools

import jax
import jax.numpy as jnp
from jax import lax
from jax.experimental import pallas as pl
from jax.experimental.pallas import tpu as pltpu
from jax.sharding import Mesh
from jax.sharding import PartitionSpec as P

LANES = 128
F32 = jnp.float32


def turned(columns):
    n = columns[0].shape[0]
    lane = lax.broadcasted_iota(jnp.int32, (n, LANES), 1)
    x = jnp.zeros((n, LANES), F32)
    for k, c in enumerate(columns):
        x = jnp.where(lane == k, c, x)
    x = jnp.concatenate([x, jnp.zeros((LANES - n, LANES), F32)], axis=0)
    x = x.T[:8, :]
    lane = lax.broadcasted_iota(jnp.int32, (1, LANES), 1)
    row = jnp.zeros((1, LANES), F32)
    for k in range(len(columns)):
        moved = pltpu.roll(x[k : k + 1], k * n, 1) if k else x[:1]
        row = jnp.where(lane // n == k, moved, row)
    return row


def chosen_at(teacher, source, z_at, n_z, shape):
    width = shape[1]
    base = ((source // 2 * n_z + z_at) * 2 + source % 2) * width
    return lax.broadcasted_iota(jnp.int32, shape, 1) + base == teacher


def share_stats(n_z, at_ref, logits_ref, teacher_ref, out_ref):
    n, rows, wide = logits_ref.shape
    half = wide // LANES
    teacher = teacher_ref[...]

    def block(s):
        return logits_ref[s].astype(F32)

    top = block(0)
    for s in range(1, n):
        top = jnp.maximum(top, block(s))
    peak = jnp.max(top, axis=1, keepdims=True)
    total = jnp.zeros((rows, wide), F32)
    spread = jnp.zeros((rows, wide), F32)
    target = jnp.zeros((rows, wide), F32)
    for s in range(n):
        z = block(s)
        below = z - peak
        e = jnp.exp(below)
        total += e
        spread += e * below
        target += jnp.where(chosen_at(teacher, s, at_ref[0], n_z, z.shape), z, 0.0)
    tile = turned([peak] + [jnp.sum(x, axis=1, keepdims=True) for x in (total, spread, target)])
    for j in range(out_ref.shape[0]):
        out_ref[j] = tile


def share_mass(n_z, at_ref, parts_ref, logits_ref, teacher_ref, eta_ref, row_ref, out_ref):
    n, rows, wide = logits_ref.shape
    parts = jnp.concatenate([parts_ref[j] for j in range(parts_ref.shape[0])], axis=0)
    tops, totals, spreads, targets = (
        pltpu.roll(parts, LANES - k * rows, 1) if k else parts for k in range(4)
    )
    peak = jnp.max(tops, axis=0, keepdims=True)
    gap = tops - peak
    scale = jnp.exp(jnp.minimum(gap, 0.0))
    total = jnp.sum(scale * totals, axis=0, keepdims=True)
    spread = jnp.sum(scale * (spreads + gap * totals), axis=0, keepdims=True)
    target = jnp.sum(targets, axis=0, keepdims=True)
    lane = lax.broadcasted_iota(jnp.int32, total.shape, 1)
    total = jnp.where(lane < rows, total, 1.0)
    eta = eta_ref[...]
    entropy = jnp.log(total) - spread / total
    cutoff = jnp.minimum(eta, jnp.sqrt(eta) * jnp.exp(-entropy))
    limit = cutoff * total
    tile = jnp.concatenate([peak, limit, target, jnp.zeros((5, LANES), F32)], axis=0)
    row_ref[...] = tile
    columns = jnp.concatenate([tile, jnp.zeros((LANES - 8, LANES), F32)], axis=0).T
    peak_c, limit_c = columns[:rows, 0:1], columns[:rows, 1:2]
    teacher = teacher_ref[...]
    mass = jnp.zeros((rows, wide), F32)
    for s in range(n):
        e = jnp.exp(logits_ref[s].astype(F32) - peak_c)
        chosen = chosen_at(teacher, s, at_ref[0], n_z, e.shape)
        mass += jnp.where((e > limit_c) | chosen, e, 0.0)
    tile = turned([jnp.sum(mass, axis=1, keepdims=True)])
    for j in range(out_ref.shape[0]):
        out_ref[j] = tile


def finish_rows(rows, at_ref, masses_ref, row_ref, out_ref):
    mass = masses_ref[0]
    for j in range(1, masses_ref.shape[0]):
        mass += masses_ref[j]
    row = row_ref[...]
    tile = jnp.concatenate([row[:3], mass, row[4:]], axis=0)
    lane = lax.broadcasted_iota(jnp.int32, tile.shape, 1)
    tile = jnp.where(lane < rows, tile, 0.0)
    per = LANES // rows
    placed = jnp.zeros_like(tile)
    for k in range(per):
        moved = pltpu.roll(tile, k * rows, 1) if k else tile
        placed = jnp.where(at_ref[0] % per == k, moved, placed)
    for j in range(out_ref.shape[0]):
        out_ref[j] = placed


def owner_at(place, n_z):
    return place % n_z * 2 + place // n_z


def turn_logits(n_z, logits_ref, zt_ref):
    rows = logits_ref.shape[0]
    mine = rows // (2 * n_z)
    per = LANES // mine
    for i in range(rows // LANES):
        owners = [owner_at(i * per + k, n_z) for k in range(per)]
        block = jnp.concatenate([logits_ref[j * mine : (j + 1) * mine, :] for j in owners], axis=0)
        zt_ref[:, i * LANES : (i + 1) * LANES] = block.astype(F32).T.astype(jnp.bfloat16)


def logit_grads(n_z, at_ref, rows_ref, zt_ref, codes_ref, grads_ref, loss_ref):
    groups = zt_ref.shape[1] // LANES
    mine = zt_ref.shape[1] // (2 * n_z)
    per = LANES // mine
    loss = [jnp.float32(0.0) for _ in range(loss_ref.shape[0])]
    lane = lax.broadcasted_iota(jnp.int32, (1, LANES), 1)
    for i in range(groups):
        tile = jnp.zeros(rows_ref.shape[1:], F32)
        codes = jnp.zeros((1, LANES), jnp.int32)
        for k in range(per):
            j = owner_at(i * per + k, n_z)
            tile += rows_ref[j]
            code = codes_ref[j // per : j // per + 1, :]
            shift = (k - j % per) * mine % LANES
            code = pltpu.roll(code, shift, 1) if shift else code
            codes = jnp.where(lane // mine == k, code, codes)
        peak, limit, target, mass = (tile[k : k + 1] for k in range(4))
        live = (codes & 1).astype(F32)
        rel = (codes >> 1) - at_ref[1]
        row_loss = live * (jnp.log(mass) + peak - target)
        for k in range(len(loss)):
            loss[k] += jnp.sum(jnp.where(lane + i * LANES == at_ref[0] + k, row_loss, 0.0))
        at = slice(i * LANES, (i + 1) * LANES)
        z = zt_ref[:, at].astype(F32)
        e = jnp.exp(z - peak)
        chosen = lax.broadcasted_iota(jnp.int32, z.shape, 0) == rel
        kept = jnp.where((e > limit) | chosen, e, 0.0)
        grads_ref[:, at] = (live * (kept / mass - chosen.astype(F32))).astype(jnp.bfloat16)
    for k in range(len(loss)):
        loss_ref[k] = loss[k]


def head_product(widths, ahead, grads_ref, hidden_ref, out_ref, held, result, in_sems, out_sems):
    starts = [sum(widths[:i]) for i in range(len(widths))]
    at = [pl.ds(s, w) for s, w in zip(starts, widths)]
    into = [
        pltpu.make_async_copy(hidden_ref.at[:, a], held.at[:, a], in_sems.at[i])
        for i, a in enumerate(at)
    ]
    out = [
        pltpu.make_async_copy(result.at[:, a], out_ref.at[:, a], out_sems.at[i])
        for i, a in enumerate(at)
    ]
    for copy in into[:ahead]:
        copy.start()
    for i, (s, w) in enumerate(zip(starts, widths)):
        into[i].wait()
        if i + ahead < len(widths):
            into[i + ahead].start()
        result[:, s : s + w] = jnp.dot(
            grads_ref[...], held[:, s : s + w], preferred_element_type=F32
        ).astype(result.dtype)
        out[i].start()
    for copy in out:
        copy.wait()


VMEM = pl.BlockSpec(memory_space=pltpu.VMEM)
SMEM = pl.BlockSpec(memory_space=pltpu.SMEM)


def call(kernel, outs, flops, *args, out_specs=None):
    moved = sum(a.size * a.dtype.itemsize for a in args) + sum(
        o.size * o.dtype.itemsize for o in jax.tree.leaves(outs)
    )
    return pl.pallas_call(
        kernel,
        out_shape=outs,
        in_specs=[SMEM if a.size < 8 else VMEM for a in args],
        out_specs=out_specs or jax.tree.map(lambda _: VMEM, outs),
        compiler_params=pltpu.CompilerParams(vmem_limit_bytes=24 << 20),
        cost_estimate=pl.CostEstimate(flops=flops, bytes_accessed=moved, transcendentals=0),
    )(*args)


def swap(parts, axis):
    return lax.all_to_all(parts, axis, split_axis=0, concat_axis=0, tiled=True)


def per_device(hidden, logits, eta, teacher, valid):
    n_z, n_vocab = lax.axis_size("z"), lax.axis_size("vocab")
    plane = ("vocab", "core")
    n_plane = 2 * n_vocab
    rows, wide = logits.shape
    width = hidden.shape[1]
    g = rows // LANES
    mine = rows // n_plane
    share = rows // (n_z * n_plane)
    shape = jax.ShapeDtypeStruct
    at_z, at_core, at_vocab = (lax.axis_index(a) for a in ("z", "core", "vocab"))
    at_plane = at_vocab * 2 + at_core

    whole = lax.all_gather(hidden, ("core", "z"), axis=0, tiled=True)

    mine_logits = swap(logits.reshape(n_plane, mine, wide), plane)
    zt = call(functools.partial(turn_logits, n_z), shape((wide, rows), jnp.bfloat16), rows * wide, logits)
    my_teacher = lax.dynamic_slice_in_dim(teacher, at_plane * mine, mine).reshape(mine, 1)
    my_eta = lax.dynamic_slice_in_dim(eta, at_plane * mine, mine)
    my_eta = jnp.pad(my_eta, (0, LANES - mine), constant_values=0.001).reshape(1, LANES)
    z_one = at_z.reshape(1)
    tiles = shape((n_z, 1, LANES), F32)
    parts = call(
        functools.partial(share_stats, n_z), tiles, 20 * rows * wide, z_one, mine_logits, my_teacher
    )
    row_stats, masses = call(
        functools.partial(share_mass, n_z),
        (shape((8, LANES), F32), tiles),
        20 * rows * wide,
        z_one,
        swap(parts, "z"),
        mine_logits,
        my_teacher,
        my_eta,
    )
    done = call(
        functools.partial(finish_rows, mine),
        shape((n_plane, 8, LANES), F32),
        rows * 16,
        (at_plane % 2 * n_z + at_plane // 2).reshape(1),
        swap(masses, "z"),
        row_stats,
    )
    done = swap(done, plane)
    codes = (teacher * 2 + valid).reshape(g, LANES)
    own = (at_core * n_z + at_z) * mine + at_vocab * share
    base = ((at_vocab * n_z + at_z) * 2 + at_core) * wide
    grads, row_loss = call(
        functools.partial(logit_grads, n_z),
        (shape((wide, rows), jnp.bfloat16), shape((share,), F32)),
        20 * rows * wide,
        jnp.stack([own, base]),
        done,
        zt,
        codes,
        out_specs=(VMEM, SMEM),
    )

    widths, left = [512], width - 512
    while left:
        widths.append(min(1024, left))
        left -= widths[-1]
    any_space = pl.BlockSpec(memory_space=pl.ANY)
    head_grad = pl.pallas_call(
        functools.partial(head_product, widths, 3),
        in_specs=[VMEM, any_space],
        out_specs=any_space,
        out_shape=shape((wide, width), jnp.bfloat16),
        scratch_shapes=[
            pltpu.VMEM((rows, width), jnp.bfloat16),
            pltpu.VMEM((wide, width), jnp.bfloat16),
            pltpu.SemaphoreType.DMA((len(widths),)),
            pltpu.SemaphoreType.DMA((len(widths),)),
        ],
        compiler_params=pltpu.CompilerParams(vmem_limit_bytes=56 << 20),
        cost_estimate=pl.CostEstimate(
            flops=2 * rows * wide * width,
            bytes_accessed=2 * (rows * width + wide * width),
            transcendentals=0,
        ),
    )(grads, whole)
    return head_grad, row_loss


def solution(mesh):
    n_rows, n_vocab = mesh.devices.shape
    split = Mesh(mesh.devices.reshape(n_rows // 2, 2, n_vocab), ("z", "core", "vocab"))
    rows, entries = ("z", "core"), ("vocab", "z", "core")
    return jax.shard_map(
        per_device,
        mesh=split,
        in_specs=(P(rows, None), P(None, entries), P(), P(), P()),
        out_specs=(P(entries, None), P(("z", "core", "vocab"))),
        check_vma=False,
    )
```

```python
import functools

import jax
import jax.numpy as jnp
from jax import lax
from jax.experimental import pallas as pl
from jax.experimental.pallas import tpu as pltpu
from jax.sharding import Mesh
from jax.sharding import PartitionSpec as P

LANES = 128
F32 = jnp.float32


def turned(columns):
    n = columns[0].shape[0]
    lane = lax.broadcasted_iota(jnp.int32, (n, LANES), 1)
    x = jnp.zeros((n, LANES), F32)
    for k, c in enumerate(columns):
        x = jnp.where(lane == k, c, x)
    x = jnp.concatenate([x, jnp.zeros((LANES - n, LANES), F32)], axis=0)
    x = x.T[:8, :]
    lane = lax.broadcasted_iota(jnp.int32, (1, LANES), 1)
    row = jnp.zeros((1, LANES), F32)
    for k in range(len(columns)):
        moved = pltpu.roll(x[k : k + 1], k * n, 1) if k else x[:1]
        row = jnp.where(lane // n == k, moved, row)
    return row


def chosen_at(teacher, source, z_at, n_z, shape):
    width = shape[1]
    base = ((source // 2 * n_z + z_at) * 2 + source % 2) * width
    return lax.broadcasted_iota(jnp.int32, shape, 1) + base == teacher


def share_stats(n_z, at_ref, logits_ref, teacher_ref, out_ref):
    n, rows, wide = logits_ref.shape
    half = wide // LANES
    teacher = teacher_ref[...]

    def block(s):
        return logits_ref[s].astype(F32)

    top = block(0)
    for s in range(1, n):
        top = jnp.maximum(top, block(s))
    peak = jnp.max(top, axis=1, keepdims=True)
    total = jnp.zeros((rows, wide), F32)
    spread = jnp.zeros((rows, wide), F32)
    target = jnp.zeros((rows, wide), F32)
    for s in range(n):
        z = block(s)
        below = z - peak
        e = jnp.exp(below)
        total += e
        spread += e * below
        target += jnp.where(chosen_at(teacher, s, at_ref[0], n_z, z.shape), z, 0.0)
    tile = turned([peak] + [jnp.sum(x, axis=1, keepdims=True) for x in (total, spread, target)])
    for j in range(out_ref.shape[0]):
        out_ref[j] = tile


def share_mass(n_z, at_ref, parts_ref, logits_ref, teacher_ref, eta_ref, row_ref, out_ref):
    n, rows, wide = logits_ref.shape
    parts = jnp.concatenate([parts_ref[j] for j in range(parts_ref.shape[0])], axis=0)
    tops, totals, spreads, targets = (
        pltpu.roll(parts, LANES - k * rows, 1) if k else parts for k in range(4)
    )
    peak = jnp.max(tops, axis=0, keepdims=True)
    gap = tops - peak
    scale = jnp.exp(jnp.minimum(gap, 0.0))
    total = jnp.sum(scale * totals, axis=0, keepdims=True)
    spread = jnp.sum(scale * (spreads + gap * totals), axis=0, keepdims=True)
    target = jnp.sum(targets, axis=0, keepdims=True)
    lane = lax.broadcasted_iota(jnp.int32, total.shape, 1)
    total = jnp.where(lane < rows, total, 1.0)
    eta = eta_ref[...]
    entropy = jnp.log(total) - spread / total
    cutoff = jnp.minimum(eta, jnp.sqrt(eta) * jnp.exp(-entropy))
    limit = cutoff * total
    tile = jnp.concatenate([peak, limit, target, jnp.zeros((5, LANES), F32)], axis=0)
    row_ref[...] = tile
    columns = jnp.concatenate([tile, jnp.zeros((LANES - 8, LANES), F32)], axis=0).T
    peak_c, limit_c = columns[:rows, 0:1], columns[:rows, 1:2]
    teacher = teacher_ref[...]
    mass = jnp.zeros((rows, wide), F32)
    for s in range(n):
        e = jnp.exp(logits_ref[s].astype(F32) - peak_c)
        chosen = chosen_at(teacher, s, at_ref[0], n_z, e.shape)
        mass += jnp.where((e > limit_c) | chosen, e, 0.0)
    tile = turned([jnp.sum(mass, axis=1, keepdims=True)])
    for j in range(out_ref.shape[0]):
        out_ref[j] = tile


def finish_rows(rows, at_ref, masses_ref, row_ref, out_ref):
    mass = masses_ref[0]
    for j in range(1, masses_ref.shape[0]):
        mass += masses_ref[j]
    row = row_ref[...]
    tile = jnp.concatenate([row[:3], mass, row[4:]], axis=0)
    lane = lax.broadcasted_iota(jnp.int32, tile.shape, 1)
    tile = jnp.where(lane < rows, tile, 0.0)
    per = LANES // rows
    placed = jnp.zeros_like(tile)
    for k in range(per):
        moved = pltpu.roll(tile, k * rows, 1) if k else tile
        placed = jnp.where(at_ref[0] % per == k, moved, placed)
    for j in range(out_ref.shape[0]):
        out_ref[j] = placed


def owner_at(place, n_z):
    return place % n_z * 2 + place // n_z


def turn_logits(n_z, logits_ref, zt_ref):
    rows = logits_ref.shape[0]
    mine = rows // (2 * n_z)
    per = LANES // mine
    for i in range(rows // LANES):
        owners = [owner_at(i * per + k, n_z) for k in range(per)]
        block = jnp.concatenate([logits_ref[j * mine : (j + 1) * mine, :] for j in owners], axis=0)
        zt_ref[:, i * LANES : (i + 1) * LANES] = block.astype(F32).T.astype(jnp.bfloat16)


def logit_grads(n_z, at_ref, rows_ref, zt_ref, codes_ref, grads_ref, loss_ref):
    groups = zt_ref.shape[1] // LANES
    mine = zt_ref.shape[1] // (2 * n_z)
    per = LANES // mine
    loss = [jnp.float32(0.0) for _ in range(loss_ref.shape[0])]
    lane = lax.broadcasted_iota(jnp.int32, (1, LANES), 1)
    for i in range(groups):
        tile = jnp.zeros(rows_ref.shape[1:], F32)
        codes = jnp.zeros((1, LANES), jnp.int32)
        for k in range(per):
            j = owner_at(i * per + k, n_z)
            tile += rows_ref[j]
            code = codes_ref[j // per : j // per + 1, :]
            shift = (k - j % per) * mine % LANES
            code = pltpu.roll(code, shift, 1) if shift else code
            codes = jnp.where(lane // mine == k, code, codes)
        peak, limit, target, mass = (tile[k : k + 1] for k in range(4))
        live = (codes & 1).astype(F32)
        rel = (codes >> 1) - at_ref[1]
        row_loss = live * (jnp.log(mass) + peak - target)
        for k in range(len(loss)):
            loss[k] += jnp.sum(jnp.where(lane + i * LANES == at_ref[0] + k, row_loss, 0.0))
        at = slice(i * LANES, (i + 1) * LANES)
        z = zt_ref[:, at].astype(F32)
        e = jnp.exp(z - peak)
        chosen = lax.broadcasted_iota(jnp.int32, z.shape, 0) == rel
        kept = jnp.where((e > limit) | chosen, e, 0.0)
        grads_ref[:, at] = (live * (kept / mass - chosen.astype(F32))).astype(jnp.bfloat16)
    for k in range(len(loss)):
        loss_ref[k] = loss[k]


def head_product(tile, grads_ref, hidden_ref, out_ref, weights, held, total, result, sems, out_sems):
    rows, width = hidden_ref.shape
    half = rows // 2
    lower, upper = pl.ds(0, half), pl.ds(half, half)
    first = pltpu.make_async_copy(hidden_ref.at[lower], held.at[lower], sems.at[0])
    second = pltpu.make_async_copy(hidden_ref.at[upper], held.at[upper], sems.at[1])
    left = pltpu.make_async_copy(grads_ref, weights, sems.at[2])
    left.start()
    first.start()
    second.start()
    starts = list(range(0, width, tile))
    left.wait()
    first.wait()
    for s in starts:
        at = slice(s, min(s + tile, width))
        total[:, at] = jnp.dot(weights[:, :half], held[:half, at], preferred_element_type=F32)
    second.wait()
    out = []
    for i, s in enumerate(starts):
        at = slice(s, min(s + tile, width))
        more = jnp.dot(weights[:, half:], held[half:, at], preferred_element_type=F32)
        result[:, at] = (total[:, at] + more).astype(result.dtype)
        part = pl.ds(s, min(tile, width - s))
        out.append(pltpu.make_async_copy(result.at[:, part], out_ref.at[:, part], out_sems.at[i]))
        out[-1].start()
    for copy in out:
        copy.wait()


VMEM = pl.BlockSpec(memory_space=pltpu.VMEM)
SMEM = pl.BlockSpec(memory_space=pltpu.SMEM)


def call(kernel, outs, flops, *args, out_specs=None):
    moved = sum(a.size * a.dtype.itemsize for a in args) + sum(
        o.size * o.dtype.itemsize for o in jax.tree.leaves(outs)
    )
    return pl.pallas_call(
        kernel,
        out_shape=outs,
        in_specs=[SMEM if a.size < 8 else VMEM for a in args],
        out_specs=out_specs or jax.tree.map(lambda _: VMEM, outs),
        compiler_params=pltpu.CompilerParams(vmem_limit_bytes=24 << 20),
        cost_estimate=pl.CostEstimate(flops=flops, bytes_accessed=moved, transcendentals=0),
    )(*args)


def swap(parts, axis):
    return lax.all_to_all(parts, axis, split_axis=0, concat_axis=0, tiled=True)


def per_device(hidden, logits, eta, teacher, valid):
    n_z, n_vocab = lax.axis_size("z"), lax.axis_size("vocab")
    plane = ("vocab", "core")
    n_plane = 2 * n_vocab
    rows, wide = logits.shape
    width = hidden.shape[1]
    g = rows // LANES
    mine = rows // n_plane
    share = rows // (n_z * n_plane)
    shape = jax.ShapeDtypeStruct
    at_z, at_core, at_vocab = (lax.axis_index(a) for a in ("z", "core", "vocab"))
    at_plane = at_vocab * 2 + at_core

    whole = lax.all_gather(hidden, ("core", "z"), axis=0, tiled=True)

    mine_logits = swap(logits.reshape(n_plane, mine, wide), plane)
    zt = call(functools.partial(turn_logits, n_z), shape((wide, rows), jnp.bfloat16), rows * wide, logits)
    my_teacher = lax.dynamic_slice_in_dim(teacher, at_plane * mine, mine).reshape(mine, 1)
    my_eta = lax.dynamic_slice_in_dim(eta, at_plane * mine, mine)
    my_eta = jnp.pad(my_eta, (0, LANES - mine), constant_values=0.001).reshape(1, LANES)
    z_one = at_z.reshape(1)
    tiles = shape((n_z, 1, LANES), F32)
    parts = call(
        functools.partial(share_stats, n_z), tiles, 20 * rows * wide, z_one, mine_logits, my_teacher
    )
    row_stats, masses = call(
        functools.partial(share_mass, n_z),
        (shape((8, LANES), F32), tiles),
        20 * rows * wide,
        z_one,
        swap(parts, "z"),
        mine_logits,
        my_teacher,
        my_eta,
    )
    done = call(
        functools.partial(finish_rows, mine),
        shape((n_plane, 8, LANES), F32),
        rows * 16,
        (at_plane % 2 * n_z + at_plane // 2).reshape(1),
        swap(masses, "z"),
        row_stats,
    )
    done = swap(done, plane)
    codes = (teacher * 2 + valid).reshape(g, LANES)
    own = (at_core * n_z + at_z) * mine + at_vocab * share
    base = ((at_vocab * n_z + at_z) * 2 + at_core) * wide
    grads, row_loss = call(
        functools.partial(logit_grads, n_z),
        (shape((wide, rows), jnp.bfloat16), shape((share,), F32)),
        20 * rows * wide,
        jnp.stack([own, base]),
        done,
        zt,
        codes,
        out_specs=(VMEM, SMEM),
    )

    tile = 768
    any_space = pl.BlockSpec(memory_space=pl.ANY)
    head_grad = pl.pallas_call(
        functools.partial(head_product, tile),
        in_specs=[any_space, any_space],
        out_specs=any_space,
        out_shape=shape((wide, width), jnp.bfloat16),
        scratch_shapes=[
            pltpu.VMEM((wide, rows), jnp.bfloat16),
            pltpu.VMEM((rows, width), jnp.bfloat16),
            pltpu.VMEM((wide, width), F32),
            pltpu.VMEM((wide, width), jnp.bfloat16),
            pltpu.SemaphoreType.DMA((3,)),
            pltpu.SemaphoreType.DMA((-(-width // tile),)),
        ],
        compiler_params=pltpu.CompilerParams(vmem_limit_bytes=56 << 20),
        cost_estimate=pl.CostEstimate(
            flops=2 * rows * wide * width,
            bytes_accessed=2 * (rows * width + wide * width),
            transcendentals=0,
        ),
    )(grads, whole)
    return head_grad, row_loss


def solution(mesh):
    n_rows, n_vocab = mesh.devices.shape
    split = Mesh(mesh.devices.reshape(n_rows // 2, 2, n_vocab), ("z", "core", "vocab"))
    rows, entries = ("z", "core"), ("vocab", "z", "core")
    return jax.shard_map(
        per_device,
        mesh=split,
        in_specs=(P(rows, None), P(None, entries), P(), P(), P()),
        out_specs=(P(entries, None), P(("z", "core", "vocab"))),
        check_vma=False,
    )
```

```python
import functools

import jax
import jax.numpy as jnp
from jax import lax
from jax.experimental import pallas as pl
from jax.experimental.pallas import tpu as pltpu
from jax.sharding import Mesh
from jax.sharding import PartitionSpec as P

LANES = 128
F32 = jnp.float32


def turned(columns):
    n = columns[0].shape[0]
    lane = lax.broadcasted_iota(jnp.int32, (n, LANES), 1)
    x = jnp.zeros((n, LANES), F32)
    for k, c in enumerate(columns):
        x = jnp.where(lane == k, c, x)
    x = jnp.concatenate([x, jnp.zeros((LANES - n, LANES), F32)], axis=0)
    x = x.T[:8, :]
    lane = lax.broadcasted_iota(jnp.int32, (1, LANES), 1)
    row = jnp.zeros((1, LANES), F32)
    for k in range(len(columns)):
        moved = pltpu.roll(x[k : k + 1], k * n, 1) if k else x[:1]
        row = jnp.where(lane // n == k, moved, row)
    return row


def chosen_at(teacher, source, z_at, n_z, shape):
    width = shape[1]
    base = ((source // 2 * n_z + z_at) * 2 + source % 2) * width
    return lax.broadcasted_iota(jnp.int32, shape, 1) + base == teacher


def share_stats(n_z, at_ref, logits_ref, teacher_ref, out_ref):
    n, rows, wide = logits_ref.shape
    half = wide // LANES
    teacher = teacher_ref[...]

    def block(s):
        return logits_ref[s].astype(F32)

    top = block(0)
    for s in range(1, n):
        top = jnp.maximum(top, block(s))
    peak = jnp.max(top, axis=1, keepdims=True)
    total = jnp.zeros((rows, wide), F32)
    spread = jnp.zeros((rows, wide), F32)
    target = jnp.zeros((rows, wide), F32)
    for s in range(n):
        z = block(s)
        below = z - peak
        e = jnp.exp(below)
        total += e
        spread += e * below
        target += jnp.where(chosen_at(teacher, s, at_ref[0], n_z, z.shape), z, 0.0)
    tile = turned([peak] + [jnp.sum(x, axis=1, keepdims=True) for x in (total, spread, target)])
    for j in range(out_ref.shape[0]):
        out_ref[j] = tile


def share_mass(n_z, at_ref, parts_ref, logits_ref, teacher_ref, eta_ref, row_ref, out_ref):
    n, rows, wide = logits_ref.shape
    parts = jnp.concatenate([parts_ref[j] for j in range(parts_ref.shape[0])], axis=0)
    tops, totals, spreads, targets = (
        pltpu.roll(parts, LANES - k * rows, 1) if k else parts for k in range(4)
    )
    peak = jnp.max(tops, axis=0, keepdims=True)
    gap = tops - peak
    scale = jnp.exp(jnp.minimum(gap, 0.0))
    total = jnp.sum(scale * totals, axis=0, keepdims=True)
    spread = jnp.sum(scale * (spreads + gap * totals), axis=0, keepdims=True)
    target = jnp.sum(targets, axis=0, keepdims=True)
    lane = lax.broadcasted_iota(jnp.int32, total.shape, 1)
    total = jnp.where(lane < rows, total, 1.0)
    eta = eta_ref[...]
    entropy = jnp.log(total) - spread / total
    cutoff = jnp.minimum(eta, jnp.sqrt(eta) * jnp.exp(-entropy))
    limit = cutoff * total
    tile = jnp.concatenate([peak, limit, target, jnp.zeros((5, LANES), F32)], axis=0)
    row_ref[...] = tile
    columns = jnp.concatenate([tile, jnp.zeros((LANES - 8, LANES), F32)], axis=0).T
    peak_c, limit_c = columns[:rows, 0:1], columns[:rows, 1:2]
    teacher = teacher_ref[...]
    mass = jnp.zeros((rows, wide), F32)
    for s in range(n):
        e = jnp.exp(logits_ref[s].astype(F32) - peak_c)
        chosen = chosen_at(teacher, s, at_ref[0], n_z, e.shape)
        mass += jnp.where((e > limit_c) | chosen, e, 0.0)
    tile = turned([jnp.sum(mass, axis=1, keepdims=True)])
    for j in range(out_ref.shape[0]):
        out_ref[j] = tile


def finish_rows(rows, masses_ref, row_ref, out_ref):
    mass = masses_ref[0]
    for j in range(1, masses_ref.shape[0]):
        mass += masses_ref[j]
    lane = lax.broadcasted_iota(jnp.int32, mass.shape, 1)
    side = jnp.zeros_like(mass)
    for k, row in enumerate([row_ref[0:1, :], row_ref[1:2, :], row_ref[2:3, :], mass]):
        moved = pltpu.roll(row, k * rows, 1) if k else row
        side = jnp.where(lane // rows == k, moved, side)
    for j in range(out_ref.shape[0]):
        out_ref[j] = side


def owner_at(place, n_z):
    return place % n_z * 2 + place // n_z


def turn_logits(n_z, logits_ref, zt_ref):
    rows = logits_ref.shape[0]
    mine = rows // (2 * n_z)
    per = LANES // mine
    for i in range(rows // LANES):
        owners = [owner_at(i * per + k, n_z) for k in range(per)]
        block = jnp.concatenate([logits_ref[j * mine : (j + 1) * mine, :] for j in owners], axis=0)
        zt_ref[:, i * LANES : (i + 1) * LANES] = block.astype(F32).T.astype(jnp.bfloat16)


def logit_grads(n_z, at_ref, rows_ref, zt_ref, codes_ref, grads_ref, loss_ref):
    groups = zt_ref.shape[1] // LANES
    mine = zt_ref.shape[1] // (2 * n_z)
    per = LANES // mine
    loss = [jnp.float32(0.0) for _ in range(loss_ref.shape[0])]
    lane = lax.broadcasted_iota(jnp.int32, (1, LANES), 1)
    for i in range(groups):
        codes = jnp.zeros((1, LANES), jnp.int32)
        stats = [jnp.ones((1, LANES), F32) for _ in range(4)]
        for k in range(per):
            j = owner_at(i * per + k, n_z)
            for q in range(4):
                shift = (k - q) * mine % LANES
                part = pltpu.roll(rows_ref[j], shift, 1) if shift else rows_ref[j]
                stats[q] = jnp.where(lane // mine == k, part, stats[q])
            code = codes_ref[j // per : j // per + 1, :]
            shift = (k - j % per) * mine % LANES
            code = pltpu.roll(code, shift, 1) if shift else code
            codes = jnp.where(lane // mine == k, code, codes)
        peak, limit, target, mass = stats
        live = (codes & 1).astype(F32)
        rel = (codes >> 1) - at_ref[1]
        row_loss = live * (jnp.log(mass) + peak - target)
        for k in range(len(loss)):
            loss[k] += jnp.sum(jnp.where(lane + i * LANES == at_ref[0] + k, row_loss, 0.0))
        at = slice(i * LANES, (i + 1) * LANES)
        z = zt_ref[:, at].astype(F32)
        e = jnp.exp(z - peak)
        chosen = lax.broadcasted_iota(jnp.int32, z.shape, 0) == rel
        kept = jnp.where((e > limit) | chosen, e, 0.0)
        grads_ref[:, at] = (live * (kept / mass - chosen.astype(F32))).astype(jnp.bfloat16)
    for k in range(len(loss)):
        loss_ref[k] = loss[k]


def head_product(tile, grads_ref, hidden_ref, out_ref, weights, held, total, result, sems, out_sems):
    rows, width = hidden_ref.shape
    half = rows // 2
    lower, upper = pl.ds(0, half), pl.ds(half, half)
    first = pltpu.make_async_copy(hidden_ref.at[lower], held.at[lower], sems.at[0])
    second = pltpu.make_async_copy(hidden_ref.at[upper], held.at[upper], sems.at[1])
    left = pltpu.make_async_copy(grads_ref, weights, sems.at[2])
    left.start()
    first.start()
    second.start()
    starts = list(range(0, width, tile))
    left.wait()
    first.wait()
    for s in starts:
        at = slice(s, min(s + tile, width))
        total[:, at] = jnp.dot(weights[:, :half], held[:half, at], preferred_element_type=F32)
    second.wait()
    out = []
    for i, s in enumerate(starts):
        at = slice(s, min(s + tile, width))
        more = jnp.dot(weights[:, half:], held[half:, at], preferred_element_type=F32)
        result[:, at] = (total[:, at] + more).astype(result.dtype)
        part = pl.ds(s, min(tile, width - s))
        out.append(pltpu.make_async_copy(result.at[:, part], out_ref.at[:, part], out_sems.at[i]))
        out[-1].start()
    for copy in out:
        copy.wait()


VMEM = pl.BlockSpec(memory_space=pltpu.VMEM)
SMEM = pl.BlockSpec(memory_space=pltpu.SMEM)


def call(kernel, outs, flops, *args, out_specs=None):
    moved = sum(a.size * a.dtype.itemsize for a in args) + sum(
        o.size * o.dtype.itemsize for o in jax.tree.leaves(outs)
    )
    return pl.pallas_call(
        kernel,
        out_shape=outs,
        in_specs=[SMEM if a.size < 8 else VMEM for a in args],
        out_specs=out_specs or jax.tree.map(lambda _: VMEM, outs),
        compiler_params=pltpu.CompilerParams(vmem_limit_bytes=24 << 20),
        cost_estimate=pl.CostEstimate(flops=flops, bytes_accessed=moved, transcendentals=0),
    )(*args)


def swap(parts, axis):
    return lax.all_to_all(parts, axis, split_axis=0, concat_axis=0, tiled=True)


def per_device(hidden, logits, eta, teacher, valid):
    n_z, n_vocab = lax.axis_size("z"), lax.axis_size("vocab")
    plane = ("vocab", "core")
    n_plane = 2 * n_vocab
    rows, wide = logits.shape
    width = hidden.shape[1]
    g = rows // LANES
    mine = rows // n_plane
    share = rows // (n_z * n_plane)
    shape = jax.ShapeDtypeStruct
    at_z, at_core, at_vocab = (lax.axis_index(a) for a in ("z", "core", "vocab"))
    at_plane = at_vocab * 2 + at_core

    whole = lax.all_gather(hidden, ("core", "z"), axis=0, tiled=True)

    mine_logits = swap(logits.reshape(n_plane, mine, wide), plane)
    zt = call(functools.partial(turn_logits, n_z), shape((wide, rows), jnp.bfloat16), rows * wide, logits)
    my_teacher = lax.dynamic_slice_in_dim(teacher, at_plane * mine, mine).reshape(mine, 1)
    my_eta = lax.dynamic_slice_in_dim(eta, at_plane * mine, mine)
    my_eta = jnp.pad(my_eta, (0, LANES - mine), constant_values=0.001).reshape(1, LANES)
    z_one = at_z.reshape(1)
    tiles = shape((n_z, 1, LANES), F32)
    parts = call(
        functools.partial(share_stats, n_z), tiles, 20 * rows * wide, z_one, mine_logits, my_teacher
    )
    row_stats, masses = call(
        functools.partial(share_mass, n_z),
        (shape((8, LANES), F32), tiles),
        20 * rows * wide,
        z_one,
        swap(parts, "z"),
        mine_logits,
        my_teacher,
        my_eta,
    )
    done = call(
        functools.partial(finish_rows, mine),
        shape((n_plane, 1, LANES), F32),
        rows * 16,
        swap(masses, "z"),
        row_stats,
    )
    done = swap(done, plane)
    codes = (teacher * 2 + valid).reshape(g, LANES)
    own = (at_core * n_z + at_z) * mine + at_vocab * share
    base = ((at_vocab * n_z + at_z) * 2 + at_core) * wide
    grads, row_loss = call(
        functools.partial(logit_grads, n_z),
        (shape((wide, rows), jnp.bfloat16), shape((share,), F32)),
        20 * rows * wide,
        jnp.stack([own, base]),
        done,
        zt,
        codes,
        out_specs=(VMEM, SMEM),
    )

    tile = 768
    any_space = pl.BlockSpec(memory_space=pl.ANY)
    head_grad = pl.pallas_call(
        functools.partial(head_product, tile),
        in_specs=[any_space, any_space],
        out_specs=any_space,
        out_shape=shape((wide, width), jnp.bfloat16),
        scratch_shapes=[
            pltpu.VMEM((wide, rows), jnp.bfloat16),
            pltpu.VMEM((rows, width), jnp.bfloat16),
            pltpu.VMEM((wide, width), F32),
            pltpu.VMEM((wide, width), jnp.bfloat16),
            pltpu.SemaphoreType.DMA((3,)),
            pltpu.SemaphoreType.DMA((-(-width // tile),)),
        ],
        compiler_params=pltpu.CompilerParams(vmem_limit_bytes=56 << 20),
        cost_estimate=pl.CostEstimate(
            flops=2 * rows * wide * width,
            bytes_accessed=2 * (rows * width + wide * width),
            transcendentals=0,
        ),
    )(grads, whole)
    return head_grad, row_loss


def solution(mesh):
    n_rows, n_vocab = mesh.devices.shape
    split = Mesh(mesh.devices.reshape(n_rows // 2, 2, n_vocab), ("z", "core", "vocab"))
    rows, entries = ("z", "core"), ("vocab", "z", "core")
    return jax.shard_map(
        per_device,
        mesh=split,
        in_specs=(P(rows, None), P(None, entries), P(), P(), P()),
        out_specs=(P(entries, None), P(("z", "core", "vocab"))),
        check_vma=False,
    )
```

```python
import functools

import jax
import jax.numpy as jnp
from jax import lax
from jax.experimental import pallas as pl
from jax.experimental.pallas import tpu as pltpu
from jax.sharding import Mesh
from jax.sharding import PartitionSpec as P

LANES = 128
F32 = jnp.float32


def turned(columns):
    n = columns[0].shape[0]
    lane = lax.broadcasted_iota(jnp.int32, (n, LANES), 1)
    x = jnp.zeros((n, LANES), F32)
    for k, c in enumerate(columns):
        x = jnp.where(lane == k, c, x)
    x = jnp.concatenate([x, jnp.zeros((LANES - n, LANES), F32)], axis=0)
    x = x.T[:8, :]
    lane = lax.broadcasted_iota(jnp.int32, (1, LANES), 1)
    row = jnp.zeros((1, LANES), F32)
    for k in range(len(columns)):
        moved = pltpu.roll(x[k : k + 1], k * n, 1) if k else x[:1]
        row = jnp.where(lane // n == k, moved, row)
    return row


def chosen_at(teacher, source, z_at, n_z, shape):
    width = shape[1]
    base = ((source // 2 * n_z + z_at) * 2 + source % 2) * width
    return lax.broadcasted_iota(jnp.int32, shape, 1) + base == teacher


def share_stats(n_z, at_ref, logits_ref, teacher_ref, out_ref):
    n, rows, wide = logits_ref.shape
    half = wide // LANES
    teacher = teacher_ref[...]

    def block(s):
        return logits_ref[s].astype(F32)

    top = block(0)
    for s in range(1, n):
        top = jnp.maximum(top, block(s))
    peak = jnp.max(top, axis=1, keepdims=True)
    total = jnp.zeros((rows, wide), F32)
    spread = jnp.zeros((rows, wide), F32)
    target = jnp.zeros((rows, wide), F32)
    for s in range(n):
        z = block(s)
        below = z - peak
        e = jnp.exp(below)
        total += e
        spread += e * below
        target += jnp.where(chosen_at(teacher, s, at_ref[0], n_z, z.shape), z, 0.0)
    tile = turned([peak] + [jnp.sum(x, axis=1, keepdims=True) for x in (total, spread, target)])
    for j in range(out_ref.shape[0]):
        out_ref[j] = tile


def share_mass(n_z, at_ref, parts_ref, logits_ref, teacher_ref, eta_ref, row_ref, out_ref):
    n, rows, wide = logits_ref.shape
    parts = jnp.concatenate([parts_ref[j] for j in range(parts_ref.shape[0])], axis=0)
    tops, totals, spreads, targets = (
        pltpu.roll(parts, LANES - k * rows, 1) if k else parts for k in range(4)
    )
    peak = jnp.max(tops, axis=0, keepdims=True)
    gap = tops - peak
    scale = jnp.exp(jnp.minimum(gap, 0.0))
    total = jnp.sum(scale * totals, axis=0, keepdims=True)
    spread = jnp.sum(scale * (spreads + gap * totals), axis=0, keepdims=True)
    target = jnp.sum(targets, axis=0, keepdims=True)
    lane = lax.broadcasted_iota(jnp.int32, total.shape, 1)
    total = jnp.where(lane < rows, total, 1.0)
    eta = eta_ref[...]
    entropy = jnp.log(total) - spread / total
    cutoff = jnp.minimum(eta, jnp.sqrt(eta) * jnp.exp(-entropy))
    limit = cutoff * total
    tile = jnp.concatenate([peak, limit, target, jnp.zeros((5, LANES), F32)], axis=0)
    row_ref[...] = tile
    columns = jnp.concatenate([tile, jnp.zeros((LANES - 8, LANES), F32)], axis=0).T
    peak_c, limit_c = columns[:rows, 0:1], columns[:rows, 1:2]
    teacher = teacher_ref[...]
    mass = jnp.zeros((rows, wide), F32)
    for s in range(n):
        e = jnp.exp(logits_ref[s].astype(F32) - peak_c)
        chosen = chosen_at(teacher, s, at_ref[0], n_z, e.shape)
        mass += jnp.where((e > limit_c) | chosen, e, 0.0)
    tile = turned([jnp.sum(mass, axis=1, keepdims=True)])
    for j in range(out_ref.shape[0]):
        out_ref[j] = tile


def finish_rows(rows, masses_ref, row_ref, out_ref):
    mass = masses_ref[0]
    for j in range(1, masses_ref.shape[0]):
        mass += masses_ref[j]
    lane = lax.broadcasted_iota(jnp.int32, mass.shape, 1)
    side = jnp.zeros_like(mass)
    for k, row in enumerate([row_ref[0:1, :], row_ref[1:2, :], row_ref[2:3, :], mass]):
        moved = pltpu.roll(row, k * rows, 1) if k else row
        side = jnp.where(lane // rows == k, moved, side)
    for j in range(out_ref.shape[0]):
        out_ref[j] = side


def owner_at(place, n_z):
    return place % n_z * 2 + place // n_z


def turn_logits(n_z, logits_ref, zt_ref):
    rows = logits_ref.shape[0]
    mine = rows // (2 * n_z)
    per = LANES // mine
    for i in range(rows // LANES):
        owners = [owner_at(i * per + k, n_z) for k in range(per)]
        block = jnp.concatenate([logits_ref[j * mine : (j + 1) * mine, :] for j in owners], axis=0)
        zt_ref[:, i * LANES : (i + 1) * LANES] = block.astype(F32).T.astype(jnp.bfloat16)


def logit_grads(n_z, at_ref, rows_ref, zt_ref, codes_ref, grads_ref, loss_ref):
    groups = zt_ref.shape[1] // LANES
    mine = zt_ref.shape[1] // (2 * n_z)
    per = LANES // mine
    loss = [jnp.float32(0.0) for _ in range(loss_ref.shape[0])]
    lane = lax.broadcasted_iota(jnp.int32, (1, LANES), 1)
    for i in range(groups):
        codes = jnp.zeros((1, LANES), jnp.int32)
        stats = [jnp.ones((1, LANES), F32) for _ in range(4)]
        for k in range(per):
            j = owner_at(i * per + k, n_z)
            for q in range(4):
                shift = (k - q) * mine % LANES
                part = pltpu.roll(rows_ref[j], shift, 1) if shift else rows_ref[j]
                stats[q] = jnp.where(lane // mine == k, part, stats[q])
            code = codes_ref[j // per : j // per + 1, :]
            shift = (k - j % per) * mine % LANES
            code = pltpu.roll(code, shift, 1) if shift else code
            codes = jnp.where(lane // mine == k, code, codes)
        peak, limit, target, mass = stats
        live = (codes & 1).astype(F32)
        rel = (codes >> 1) - at_ref[1]
        row_loss = live * (jnp.log(mass) + peak - target)
        for k in range(len(loss)):
            loss[k] += jnp.sum(jnp.where(lane + i * LANES == at_ref[0] + k, row_loss, 0.0))
        at = slice(i * LANES, (i + 1) * LANES)
        z = zt_ref[:, at].astype(F32)
        e = jnp.exp(z - peak)
        chosen = lax.broadcasted_iota(jnp.int32, z.shape, 0) == rel
        kept = jnp.where((e > limit) | chosen, e, 0.0)
        grads_ref[:, at] = (live * (kept / mass - chosen.astype(F32))).astype(jnp.bfloat16)
    for k in range(len(loss)):
        loss_ref[k] = loss[k]


def head_product(tile, grads_ref, hidden_ref, out_ref, held, total, result, sems, out_sems):
    rows, width = hidden_ref.shape
    half = rows // 2
    lower, upper = pl.ds(0, half), pl.ds(half, half)
    first = pltpu.make_async_copy(hidden_ref.at[lower], held.at[lower], sems.at[0])
    second = pltpu.make_async_copy(hidden_ref.at[upper], held.at[upper], sems.at[1])
    first.start()
    second.start()
    starts = list(range(0, width, tile))
    first.wait()
    for s in starts:
        at = slice(s, min(s + tile, width))
        total[:, at] = jnp.dot(grads_ref[:, :half], held[:half, at], preferred_element_type=F32)
    second.wait()
    out = []
    for i, s in enumerate(starts):
        at = slice(s, min(s + tile, width))
        more = jnp.dot(grads_ref[:, half:], held[half:, at], preferred_element_type=F32)
        result[:, at] = (total[:, at] + more).astype(result.dtype)
        part = pl.ds(s, min(tile, width - s))
        out.append(pltpu.make_async_copy(result.at[:, part], out_ref.at[:, part], out_sems.at[i]))
        out[-1].start()
    for copy in out:
        copy.wait()


VMEM = pl.BlockSpec(memory_space=pltpu.VMEM)
SMEM = pl.BlockSpec(memory_space=pltpu.SMEM)


def call(kernel, outs, flops, *args, out_specs=None):
    moved = sum(a.size * a.dtype.itemsize for a in args) + sum(
        o.size * o.dtype.itemsize for o in jax.tree.leaves(outs)
    )
    return pl.pallas_call(
        kernel,
        out_shape=outs,
        in_specs=[SMEM if a.size < 8 else VMEM for a in args],
        out_specs=out_specs or jax.tree.map(lambda _: VMEM, outs),
        compiler_params=pltpu.CompilerParams(vmem_limit_bytes=24 << 20),
        cost_estimate=pl.CostEstimate(flops=flops, bytes_accessed=moved, transcendentals=0),
    )(*args)


def swap(parts, axis):
    return lax.all_to_all(parts, axis, split_axis=0, concat_axis=0, tiled=True)


def per_device(hidden, logits, eta, teacher, valid):
    n_z, n_vocab = lax.axis_size("z"), lax.axis_size("vocab")
    plane = ("vocab", "core")
    n_plane = 2 * n_vocab
    rows, wide = logits.shape
    width = hidden.shape[1]
    g = rows // LANES
    mine = rows // n_plane
    share = rows // (n_z * n_plane)
    shape = jax.ShapeDtypeStruct
    at_z, at_core, at_vocab = (lax.axis_index(a) for a in ("z", "core", "vocab"))
    at_plane = at_vocab * 2 + at_core

    whole = lax.all_gather(hidden, ("core", "z"), axis=0, tiled=True)

    mine_logits = swap(logits.reshape(n_plane, mine, wide), plane)
    zt = call(functools.partial(turn_logits, n_z), shape((wide, rows), jnp.bfloat16), rows * wide, logits)
    my_teacher = lax.dynamic_slice_in_dim(teacher, at_plane * mine, mine).reshape(mine, 1)
    my_eta = lax.dynamic_slice_in_dim(eta, at_plane * mine, mine)
    my_eta = jnp.pad(my_eta, (0, LANES - mine), constant_values=0.001).reshape(1, LANES)
    z_one = at_z.reshape(1)
    tiles = shape((n_z, 1, LANES), F32)
    parts = call(
        functools.partial(share_stats, n_z), tiles, 20 * rows * wide, z_one, mine_logits, my_teacher
    )
    row_stats, masses = call(
        functools.partial(share_mass, n_z),
        (shape((8, LANES), F32), tiles),
        20 * rows * wide,
        z_one,
        swap(parts, "z"),
        mine_logits,
        my_teacher,
        my_eta,
    )
    done = call(
        functools.partial(finish_rows, mine),
        shape((n_plane, 1, LANES), F32),
        rows * 16,
        swap(masses, "z"),
        row_stats,
    )
    done = swap(done, plane)
    codes = (teacher * 2 + valid).reshape(g, LANES)
    own = (at_core * n_z + at_z) * mine + at_vocab * share
    base = ((at_vocab * n_z + at_z) * 2 + at_core) * wide
    grads, row_loss = call(
        functools.partial(logit_grads, n_z),
        (shape((wide, rows), jnp.bfloat16), shape((share,), F32)),
        20 * rows * wide,
        jnp.stack([own, base]),
        done,
        zt,
        codes,
        out_specs=(VMEM, SMEM),
    )

    tile = 512
    any_space = pl.BlockSpec(memory_space=pl.ANY)
    head_grad = pl.pallas_call(
        functools.partial(head_product, tile),
        in_specs=[VMEM, any_space],
        out_specs=any_space,
        out_shape=shape((wide, width), jnp.bfloat16),
        scratch_shapes=[
            pltpu.VMEM((rows, width), jnp.bfloat16),
            pltpu.VMEM((wide, width), F32),
            pltpu.VMEM((wide, width), jnp.bfloat16),
            pltpu.SemaphoreType.DMA((2,)),
            pltpu.SemaphoreType.DMA((-(-width // tile),)),
        ],
        compiler_params=pltpu.CompilerParams(vmem_limit_bytes=44 << 20),
        cost_estimate=pl.CostEstimate(
            flops=2 * rows * wide * width,
            bytes_accessed=2 * (rows * width + wide * width),
            transcendentals=0,
        ),
    )(grads, whole)
    return head_grad, row_loss


def solution(mesh):
    n_rows, n_vocab = mesh.devices.shape
    split = Mesh(mesh.devices.reshape(n_rows // 2, 2, n_vocab), ("z", "core", "vocab"))
    rows, entries = ("z", "core"), ("vocab", "z", "core")
    return jax.shard_map(
        per_device,
        mesh=split,
        in_specs=(P(rows, None), P(None, entries), P(), P(), P()),
        out_specs=(P(entries, None), P(("z", "core", "vocab"))),
        check_vma=False,
    )
```

```python
import functools

import jax
import jax.numpy as jnp
from jax import lax
from jax.experimental import pallas as pl
from jax.experimental.pallas import tpu as pltpu
from jax.sharding import Mesh
from jax.sharding import PartitionSpec as P

LANES = 128
F32 = jnp.float32


def turned(columns):
    n = columns[0].shape[0]
    lane = lax.broadcasted_iota(jnp.int32, (n, LANES), 1)
    x = jnp.zeros((n, LANES), F32)
    for k, c in enumerate(columns):
        x = jnp.where(lane == k, c, x)
    x = jnp.concatenate([x, jnp.zeros((LANES - n, LANES), F32)], axis=0)
    x = x.T[:8, :]
    lane = lax.broadcasted_iota(jnp.int32, (1, LANES), 1)
    row = jnp.zeros((1, LANES), F32)
    for k in range(len(columns)):
        moved = pltpu.roll(x[k : k + 1], k * n, 1) if k else x[:1]
        row = jnp.where(lane // n == k, moved, row)
    return row


def chosen_at(teacher, source, z_at, n_z, shape):
    width = shape[1]
    base = ((source // 2 * n_z + z_at) * 2 + source % 2) * width
    return lax.broadcasted_iota(jnp.int32, shape, 1) + base == teacher


def share_stats(n_z, at_ref, logits_ref, teacher_ref, out_ref):
    n, rows, wide = logits_ref.shape
    half = wide // LANES
    teacher = teacher_ref[...]

    def block(s):
        return logits_ref[s].astype(F32)

    top = block(0)
    for s in range(1, n):
        top = jnp.maximum(top, block(s))
    peak = jnp.max(top, axis=1, keepdims=True)
    total = jnp.zeros((rows, wide), F32)
    spread = jnp.zeros((rows, wide), F32)
    target = jnp.zeros((rows, wide), F32)
    for s in range(n):
        z = block(s)
        below = z - peak
        e = jnp.exp(below)
        total += e
        spread += e * below
        target += jnp.where(chosen_at(teacher, s, at_ref[0], n_z, z.shape), z, 0.0)
    tile = turned([peak] + [jnp.sum(x, axis=1, keepdims=True) for x in (total, spread, target)])
    for j in range(out_ref.shape[0]):
        out_ref[j] = tile


def share_mass(n_z, at_ref, parts_ref, logits_ref, teacher_ref, eta_ref, row_ref, out_ref):
    n, rows, wide = logits_ref.shape
    parts = jnp.concatenate([parts_ref[j] for j in range(parts_ref.shape[0])], axis=0)
    tops, totals, spreads, targets = (
        pltpu.roll(parts, LANES - k * rows, 1) if k else parts for k in range(4)
    )
    peak = jnp.max(tops, axis=0, keepdims=True)
    gap = tops - peak
    scale = jnp.exp(jnp.minimum(gap, 0.0))
    total = jnp.sum(scale * totals, axis=0, keepdims=True)
    spread = jnp.sum(scale * (spreads + gap * totals), axis=0, keepdims=True)
    target = jnp.sum(targets, axis=0, keepdims=True)
    lane = lax.broadcasted_iota(jnp.int32, total.shape, 1)
    total = jnp.where(lane < rows, total, 1.0)
    eta = eta_ref[...]
    entropy = jnp.log(total) - spread / total
    cutoff = jnp.minimum(eta, jnp.sqrt(eta) * jnp.exp(-entropy))
    limit = cutoff * total
    tile = jnp.concatenate([peak, limit, target, jnp.zeros((5, LANES), F32)], axis=0)
    row_ref[...] = tile
    columns = jnp.concatenate([tile, jnp.zeros((LANES - 8, LANES), F32)], axis=0).T
    peak_c, limit_c = columns[:rows, 0:1], columns[:rows, 1:2]
    teacher = teacher_ref[...]
    mass = jnp.zeros((rows, wide), F32)
    for s in range(n):
        e = jnp.exp(logits_ref[s].astype(F32) - peak_c)
        chosen = chosen_at(teacher, s, at_ref[0], n_z, e.shape)
        mass += jnp.where((e > limit_c) | chosen, e, 0.0)
    tile = turned([jnp.sum(mass, axis=1, keepdims=True)])
    for j in range(out_ref.shape[0]):
        out_ref[j] = tile


def finish_rows(rows, masses_ref, row_ref, out_ref):
    mass = masses_ref[0]
    for j in range(1, masses_ref.shape[0]):
        mass += masses_ref[j]
    lane = lax.broadcasted_iota(jnp.int32, mass.shape, 1)
    side = jnp.zeros_like(mass)
    for k, row in enumerate([row_ref[0:1, :], row_ref[1:2, :], row_ref[2:3, :], mass]):
        moved = pltpu.roll(row, k * rows, 1) if k else row
        side = jnp.where(lane // rows == k, moved, side)
    for j in range(out_ref.shape[0]):
        out_ref[j] = side


def owner_at(place, n_z):
    return place % n_z * 2 + place // n_z


def turn_logits(n_z, logits_ref, zt_ref):
    rows = logits_ref.shape[0]
    mine = rows // (2 * n_z)
    per = LANES // mine
    for i in range(rows // LANES):
        owners = [owner_at(i * per + k, n_z) for k in range(per)]
        block = jnp.concatenate([logits_ref[j * mine : (j + 1) * mine, :] for j in owners], axis=0)
        zt_ref[:, i * LANES : (i + 1) * LANES] = block.astype(F32).T.astype(jnp.bfloat16)


def logit_grads(n_z, at_ref, rows_ref, zt_ref, codes_ref, grads_ref, loss_ref):
    groups = zt_ref.shape[1] // LANES
    mine = zt_ref.shape[1] // (2 * n_z)
    per = LANES // mine
    loss = [jnp.float32(0.0) for _ in range(loss_ref.shape[0])]
    lane = lax.broadcasted_iota(jnp.int32, (1, LANES), 1)
    for i in range(groups):
        codes = jnp.zeros((1, LANES), jnp.int32)
        stats = [jnp.ones((1, LANES), F32) for _ in range(4)]
        for k in range(per):
            j = owner_at(i * per + k, n_z)
            for q in range(4):
                shift = (k - q) * mine % LANES
                part = pltpu.roll(rows_ref[j], shift, 1) if shift else rows_ref[j]
                stats[q] = jnp.where(lane // mine == k, part, stats[q])
            code = codes_ref[j // per : j // per + 1, :]
            shift = (k - j % per) * mine % LANES
            code = pltpu.roll(code, shift, 1) if shift else code
            codes = jnp.where(lane // mine == k, code, codes)
        peak, limit, target, mass = stats
        live = (codes & 1).astype(F32)
        rel = (codes >> 1) - at_ref[1]
        row_loss = live * (jnp.log(mass) + peak - target)
        for k in range(len(loss)):
            loss[k] += jnp.sum(jnp.where(lane + i * LANES == at_ref[0] + k, row_loss, 0.0))
        at = slice(i * LANES, (i + 1) * LANES)
        z = zt_ref[:, at].astype(F32)
        e = jnp.exp(z - peak)
        chosen = lax.broadcasted_iota(jnp.int32, z.shape, 0) == rel
        kept = jnp.where((e > limit) | chosen, e, 0.0)
        grads_ref[:, at] = (live * (kept / mass - chosen.astype(F32))).astype(jnp.bfloat16)
    for k in range(len(loss)):
        loss_ref[k] = loss[k]


def head_product(tile, grads_ref, hidden_ref, out_ref, held, total, result, sems, out_sems):
    rows, width = hidden_ref.shape
    half = rows // 2
    lower, upper = pl.ds(0, half), pl.ds(half, half)
    first = pltpu.make_async_copy(hidden_ref.at[lower], held.at[lower], sems.at[0])
    second = pltpu.make_async_copy(hidden_ref.at[upper], held.at[upper], sems.at[1])
    first.start()
    second.start(priority=1)
    starts = list(range(0, width, tile))
    first.wait()
    for s in starts:
        at = slice(s, min(s + tile, width))
        total[:, at] = jnp.dot(grads_ref[:, :half], held[:half, at], preferred_element_type=F32)
    second.wait()
    out = []
    for i, s in enumerate(starts):
        at = slice(s, min(s + tile, width))
        more = jnp.dot(grads_ref[:, half:], held[half:, at], preferred_element_type=F32)
        result[:, at] = (total[:, at] + more).astype(result.dtype)
        part = pl.ds(s, min(tile, width - s))
        out.append(pltpu.make_async_copy(result.at[:, part], out_ref.at[:, part], out_sems.at[i]))
        out[-1].start()
    for copy in out:
        copy.wait()


VMEM = pl.BlockSpec(memory_space=pltpu.VMEM)
SMEM = pl.BlockSpec(memory_space=pltpu.SMEM)


def call(kernel, outs, flops, *args, out_specs=None):
    moved = sum(a.size * a.dtype.itemsize for a in args) + sum(
        o.size * o.dtype.itemsize for o in jax.tree.leaves(outs)
    )
    return pl.pallas_call(
        kernel,
        out_shape=outs,
        in_specs=[SMEM if a.size < 8 else VMEM for a in args],
        out_specs=out_specs or jax.tree.map(lambda _: VMEM, outs),
        compiler_params=pltpu.CompilerParams(vmem_limit_bytes=24 << 20),
        cost_estimate=pl.CostEstimate(flops=flops, bytes_accessed=moved, transcendentals=0),
    )(*args)


def swap(parts, axis):
    return lax.all_to_all(parts, axis, split_axis=0, concat_axis=0, tiled=True)


def per_device(hidden, logits, eta, teacher, valid):
    n_z, n_vocab = lax.axis_size("z"), lax.axis_size("vocab")
    plane = ("vocab", "core")
    n_plane = 2 * n_vocab
    rows, wide = logits.shape
    width = hidden.shape[1]
    g = rows // LANES
    mine = rows // n_plane
    share = rows // (n_z * n_plane)
    shape = jax.ShapeDtypeStruct
    at_z, at_core, at_vocab = (lax.axis_index(a) for a in ("z", "core", "vocab"))
    at_plane = at_vocab * 2 + at_core

    whole = lax.all_gather(hidden, ("core", "z"), axis=0, tiled=True)

    mine_logits = swap(logits.reshape(n_plane, mine, wide), plane)
    zt = call(functools.partial(turn_logits, n_z), shape((wide, rows), jnp.bfloat16), rows * wide, logits)
    my_teacher = lax.dynamic_slice_in_dim(teacher, at_plane * mine, mine).reshape(mine, 1)
    my_eta = lax.dynamic_slice_in_dim(eta, at_plane * mine, mine)
    my_eta = jnp.pad(my_eta, (0, LANES - mine), constant_values=0.001).reshape(1, LANES)
    z_one = at_z.reshape(1)
    tiles = shape((n_z, 1, LANES), F32)
    parts = call(
        functools.partial(share_stats, n_z), tiles, 20 * rows * wide, z_one, mine_logits, my_teacher
    )
    row_stats, masses = call(
        functools.partial(share_mass, n_z),
        (shape((8, LANES), F32), tiles),
        20 * rows * wide,
        z_one,
        swap(parts, "z"),
        mine_logits,
        my_teacher,
        my_eta,
    )
    done = call(
        functools.partial(finish_rows, mine),
        shape((n_plane, 1, LANES), F32),
        rows * 16,
        swap(masses, "z"),
        row_stats,
    )
    done = swap(done, plane)
    codes = (teacher * 2 + valid).reshape(g, LANES)
    own = (at_core * n_z + at_z) * mine + at_vocab * share
    base = ((at_vocab * n_z + at_z) * 2 + at_core) * wide
    grads, row_loss = call(
        functools.partial(logit_grads, n_z),
        (shape((wide, rows), jnp.bfloat16), shape((share,), F32)),
        20 * rows * wide,
        jnp.stack([own, base]),
        done,
        zt,
        codes,
        out_specs=(VMEM, SMEM),
    )

    tile = 512
    any_space = pl.BlockSpec(memory_space=pl.ANY)
    head_grad = pl.pallas_call(
        functools.partial(head_product, tile),
        in_specs=[VMEM, any_space],
        out_specs=any_space,
        out_shape=shape((wide, width), jnp.bfloat16),
        scratch_shapes=[
            pltpu.VMEM((rows, width), jnp.bfloat16),
            pltpu.VMEM((wide, width), F32),
            pltpu.VMEM((wide, width), jnp.bfloat16),
            pltpu.SemaphoreType.DMA((2,)),
            pltpu.SemaphoreType.DMA((-(-width // tile),)),
        ],
        compiler_params=pltpu.CompilerParams(vmem_limit_bytes=44 << 20),
        cost_estimate=pl.CostEstimate(
            flops=2 * rows * wide * width,
            bytes_accessed=2 * (rows * width + wide * width),
            transcendentals=0,
        ),
    )(grads, whole)
    return head_grad, row_loss


def solution(mesh):
    n_rows, n_vocab = mesh.devices.shape
    split = Mesh(mesh.devices.reshape(n_rows // 2, 2, n_vocab), ("z", "core", "vocab"))
    rows, entries = ("z", "core"), ("vocab", "z", "core")
    return jax.shard_map(
        per_device,
        mesh=split,
        in_specs=(P(rows, None), P(None, entries), P(), P(), P()),
        out_specs=(P(entries, None), P(("z", "core", "vocab"))),
        check_vma=False,
    )
```
